32 devices in a mesh: dom: 4 (over y, core), shard: 8 (over z, x).
Axes of the slice: x: 2, y: 2, z: 4, core: 2. Of those that a mesh axis runs over, the one named last changes fastest.
Arguments:
- features: bfloat16 [8192, 512], P(('dom', 'shard')), may hold values from -6 to 6
- w_self: bfloat16 [512, 512], replicated, may hold values from -0.25 to 0.25
- w_neigh: bfloat16 [512, 512], replicated, may hold values from -0.25 to 0.25
- cotangent: bfloat16 [8192, 512], P(('dom', 'shard')), may hold values from -6 to 6
- neighbours: int32 [8192, 32], P(('dom', 'shard')), may hold values from 0 to 320, as said below
- hub_slots: int32 [32], P(('dom', 'shard')), may hold values from 0 to 255, as said below
- send_rows: int32 [32, 8, 4], P(('dom', 'shard')), may hold values from 0 to 255, as said below
- send_counts: int32 [32, 8], P(('dom', 'shard')), may hold values from 1 to 4, as said below
Outputs:
- hidden: bfloat16 [8192, 512], P(('dom', 'shard'))
- grad_features: float32 [8192, 512], P(('dom', 'shard'))
- grad_self: float32 [512, 512], replicated
- grad_neigh: float32 [512, 512], replicated
The draws below stay inside these ranges and needn't reach their ends.
Inputs may be any that keep to these rules, and one draw needn't show every extreme that they name: `neighbours`: padding slots (320) come after a vertex's live slots; each vertex has 4 to 32 live slots. A slot at or above 288 names peer p and position k with k below send_counts of that peer for this device. Hub indices are skewed: some hubs are read far more than others. `hub_slots`: the 1 entries of one device are distinct local rows. `send_rows`: rows may repeat; entries at or past a peer's count are not live. `send_counts`: in every partition group one shard index receives 4 rows from every peer.
All inputs are finite; a program needn't handle non-finite values.
Results may differ from the reference program's by a relative error of at most 0.0052.
Values may be sent and summed in bfloat16 or wider, within the bound.
A program may use at most 64 MiB of HBM per device.

```python
import jax
import jax.numpy as jnp
from jax import lax

F = 512
V_DEV = 256
DEG = 32
HUB_DEV = 1
CAP = 4
HUBS = 32
TOTAL_V = 8192
TABLE = 320
N_DOM = 4
N_SHARD = 8


def count_table(key):
    base_key, target_key = jax.random.split(jax.random.fold_in(key, 11))
    senders = N_DOM * N_SHARD
    base = jax.random.randint(base_key, (senders, N_SHARD), 1, CAP + 1)
    target = jax.random.randint(target_key, (N_DOM,), 0, N_SHARD)
    dom_of = jnp.arange(senders) // N_SHARD
    full = jnp.arange(N_SHARD)[None, :] == target[dom_of][:, None]
    return jnp.where(full, CAP, base).astype(jnp.int32)


def draw_send_counts(key, part):
    return count_table(key)


def draw_send_rows(key, part):
    return jax.random.randint(jax.random.fold_in(key, 23), (N_DOM * N_SHARD, N_SHARD, CAP), 0, V_DEV).astype(jnp.int32)


def draw_hub_slots(key, part):
    stride = V_DEV // HUB_DEV
    within = jnp.arange(HUBS) % HUB_DEV
    jitter = jax.random.randint(jax.random.fold_in(key, 31), (HUBS,), 0, stride)
    return (within * stride + jitter).astype(jnp.int32)


def draw_neighbours(key, part):
    total = V_DEV * N_DOM * N_SHARD
    counts = count_table(key)
    keys = jax.random.split(jax.random.fold_in(key, 47), 9)
    shape = (total, DEG)
    degree = jax.random.randint(keys[0], (total, 1), 4, DEG + 1)
    kind = jax.random.randint(keys[1], shape, 0, 10)
    local = jax.random.randint(keys[2], shape, 0, V_DEV)
    offset = jax.random.randint(keys[3], (), 0, HUBS)
    favour = (offset + jax.random.randint(keys[4], shape, 0, 16) * max(1, HUBS // 16)) % HUBS
    spread = jax.random.randint(keys[5], shape, 0, HUBS)
    coin = jax.random.randint(keys[6], shape, 0, 2)
    hub = jnp.where(coin == 0, favour, spread) + V_DEV
    peer = jax.random.randint(keys[7], shape, 0, N_SHARD)
    device = jnp.arange(total) // V_DEV
    group = device // N_SHARD
    place = device % N_SHARD
    sender = group[:, None] * N_SHARD + peer
    limit = counts[sender, place[:, None]]
    within = jax.random.randint(keys[8], shape, 0, 1 << 20) % limit
    bound = V_DEV + HUBS + peer * CAP + within
    value = jnp.where(kind < 4, local, jnp.where(kind < 7, hub, bound))
    slot = jnp.arange(DEG)[None, :]
    return jnp.where(slot < degree, value, TABLE).astype(jnp.int32)


def shard_levels(stream_key, extent, cuts, smallest, top_value):
    def one(position, shards_of):
        draws = jax.random.uniform(jax.random.fold_in(jax.random.fold_in(stream_key, 6), position), (shards_of,), jnp.float32, smallest / len(cuts), top_value / len(cuts))
        return jnp.repeat(jnp.exp(draws), extent[position] // shards_of).reshape((-1,) + (1,) * (len(extent) - position - 1))

    gain = one(*cuts[0])
    for cut in cuts[1:]:
        gain = gain * one(*cut)
    return gain


def noise(own_key, shape, scale, most, cuts=(), kind=jnp.bfloat16):
    entries = scale * jax.random.normal(own_key, shape, jnp.float32)
    if cuts:
        entries = entries * shard_levels(own_key, shape, cuts, -0.22, 0.18)
    return jnp.clip(entries, -most, most).astype(kind)


def setup_inputs(seed: int = 0) -> dict:
    key_of = jax.random.split(jax.random.key(seed), 9)
    features = noise(key_of[0], (TOTAL_V, F), 1.0, 6.0, ((0, 32),))
    w_self = noise(key_of[1], (F, F), F ** -0.5, 0.25)
    w_neigh = noise(key_of[2], (F, F), F ** -0.5, 0.25)
    cotangent = noise(key_of[3], (TOTAL_V, F), 1.0, 6.0, ((0, 32),))
    neighbours = draw_neighbours(jax.random.fold_in(key_of[8], 71), 0)
    hub_slots = draw_hub_slots(jax.random.fold_in(key_of[8], 71), 0)
    send_rows = draw_send_rows(jax.random.fold_in(key_of[8], 71), 0)
    send_counts = draw_send_counts(jax.random.fold_in(key_of[8], 71), 0)
    return {"features": features, "w_self": w_self, "w_neigh": w_neigh, "cotangent": cotangent, "neighbours": neighbours, "hub_slots": hub_slots, "send_rows": send_rows, "send_counts": send_counts}


def sources(neighbours, hub_slots, send_rows, send_counts):
    total = V_DEV * N_DOM * N_SHARD
    rows = jnp.arange(total, dtype=jnp.int32)[:, None]
    device = rows // V_DEV
    group = device // N_SHARD
    place = device % N_SHARD
    slot = neighbours
    local_src = device * V_DEV + slot
    hub_index = jnp.clip(slot - V_DEV, 0, HUBS - 1)
    hub_src = (hub_index // HUB_DEV) * V_DEV + hub_slots[hub_index]
    bound = jnp.clip(slot - V_DEV - HUBS, 0, N_SHARD * CAP - 1)
    peer = bound // CAP
    within = bound % CAP
    sender = group * N_SHARD + peer
    live = within < send_counts[sender, place]
    bound_src = jnp.where(live, sender * V_DEV + send_rows[sender, place, within], total)
    src = jnp.where(slot < V_DEV, local_src, jnp.where(slot < V_DEV + HUBS, hub_src, jnp.where(slot < TABLE, bound_src, total)))
    return src.astype(jnp.int32)


def reference(features, w_self, w_neigh, cotangent, neighbours, hub_slots, send_rows, send_counts):
    total = V_DEV * N_DOM * N_SHARD
    width = features.shape[1]
    src = sources(neighbours, hub_slots, send_rows, send_counts)
    degree = jnp.sum(neighbours < TABLE, axis=1).astype(jnp.float32)
    padded = jnp.concatenate([features, jnp.zeros((1, width), jnp.bfloat16)], axis=0)
    blocks = src.reshape(total // V_DEV, V_DEV, DEG)
    sums = lax.map(lambda blk: jnp.sum(padded[blk], axis=1, dtype=jnp.float32), blocks).reshape(total, width)
    agg = (sums / degree[:, None]).astype(jnp.bfloat16)
    z = jnp.dot(features, w_self, preferred_element_type=jnp.float32) + jnp.dot(agg, w_neigh, preferred_element_type=jnp.float32)
    sig = jax.nn.sigmoid(z)
    hidden = (z * sig).astype(jnp.bfloat16)
    dz = (cotangent.astype(jnp.float32) * sig * (1.0 + z * (1.0 - sig))).astype(jnp.bfloat16)
    grad_self = jnp.dot(features.T, dz, preferred_element_type=jnp.float32)
    grad_neigh = jnp.dot(agg.T, dz, preferred_element_type=jnp.float32)
    edge_grad = jnp.dot(dz, w_neigh.T, preferred_element_type=jnp.float32) / degree[:, None]
    grads = edge_grad.reshape(total // V_DEV, V_DEV, width)

    def add_block(acc, pair):
        blk, grad = pair
        spread = jnp.broadcast_to(grad[:, None, :], (V_DEV, DEG, width)).reshape(-1, width)
        return acc.at[blk.reshape(-1)].add(spread), None

    start = jnp.zeros((total + 1, width), jnp.float32)
    accum, _ = lax.scan(add_block, start, (blocks, grads))
    grad_features = jnp.dot(dz, w_self.T, preferred_element_type=jnp.float32) + accum[:total]
    return hidden, grad_features, grad_self, grad_neigh
```

```python
import jax
import jax.numpy as jnp
from jax import lax
from jax.sharding import PartitionSpec as P

BF = jnp.bfloat16


def contract_rows(left, right):
    return lax.dot_general(
        left, right, (((0,), (0,)), ((), ())), preferred_element_type=jnp.float32
    )


def contract_cols(left, right):
    return lax.dot_general(
        left, right, (((1,), (1,)), ((), ())), preferred_element_type=jnp.float32
    )


def body(features, w_self, w_neigh, cotangent, neighbours, hub_slots, send_rows, send_counts):
    verts, width = features.shape
    slots = neighbours.shape[1]
    peers = lax.axis_size("shard")
    devices = peers * lax.axis_size("dom")
    routes = send_rows[0]
    counts = send_counts[0]
    cap = routes.shape[1]
    live = jnp.arange(cap)[None, :] < counts[:, None]
    hubs_own = hub_slots.shape[0]
    hub_count = hubs_own * devices
    picks = jnp.concatenate([hub_slots, jnp.where(live, routes, verts).reshape(-1)])
    pick = (picks[:, None] == jnp.arange(verts)[None, :]).astype(BF)
    picked = jnp.dot(pick, features, preferred_element_type=jnp.float32).astype(BF)
    hubs = lax.all_gather(picked[:hubs_own], ("dom", "shard"), axis=0, tiled=True)
    outgoing = picked[hubs_own:].reshape(peers, cap, width)
    incoming = lax.all_to_all(outgoing, "shard", split_axis=0, concat_axis=0, tiled=True)
    table_size = verts + hub_count + peers * cap
    table = jnp.concatenate([features, hubs, incoming.reshape(peers * cap, width)], axis=0)
    degree = jnp.sum(neighbours < table_size, axis=1).astype(jnp.float32)
    names = jnp.arange(table_size)[None, :]
    count = jnp.zeros((verts, table_size), jnp.float32)
    for j in range(slots):
        count = count + (neighbours[:, j : j + 1] == names)
    count = count.astype(BF)
    sums = jnp.dot(count, table, preferred_element_type=jnp.float32)
    agg = (sums / degree[:, None]).astype(BF)
    z = jnp.dot(features, w_self, preferred_element_type=jnp.float32) + jnp.dot(
        agg, w_neigh, preferred_element_type=jnp.float32
    )
    sig = jax.nn.sigmoid(z)
    hidden = (z * sig).astype(BF)
    dz = (cotangent.astype(jnp.float32) * sig * (1.0 + z * (1.0 - sig))).astype(BF)
    both = jnp.concatenate([contract_rows(features, dz), contract_rows(agg, dz)], axis=0).astype(BF)
    parts = lax.all_to_all(
        both.reshape(devices, -1, width), ("dom", "shard"), split_axis=0, concat_axis=0, tiled=True
    )
    mine = jnp.sum(parts.astype(jnp.float32), axis=0).astype(BF)
    edge_grad = (contract_cols(dz, w_neigh) / degree[:, None]).astype(BF)
    accum = contract_rows(count, edge_grad)
    hub_part = accum[verts : verts + hub_count]
    hub_back = lax.psum_scatter(hub_part, ("dom", "shard"), scatter_dimension=0, tiled=True)
    recv_part = accum[verts + hub_count :].reshape(peers, cap, width)
    returned = lax.all_to_all(recv_part.astype(BF), "shard", split_axis=0, concat_axis=0, tiled=True)
    back = jnp.concatenate([hub_back.astype(BF), returned.reshape(-1, width)], axis=0)
    grad_features = contract_cols(dz, w_self) + accum[:verts] + contract_rows(pick, back)
    total = lax.all_gather(mine, ("dom", "shard"), axis=0, tiled=True).astype(jnp.float32)
    return (hidden, grad_features, total[:width], total[width:])


def solution(mesh):
    return jax.shard_map(
        body,
        mesh=mesh,
        in_specs=(
            P(("dom", "shard"), None),
            P(),
            P(),
            P(("dom", "shard"), None),
            P(("dom", "shard"), None),
            P(("dom", "shard")),
            P(("dom", "shard"), None, None),
            P(("dom", "shard"), None),
        ),
        out_specs=(P(("dom", "shard"), None), P(("dom", "shard"), None), P(), P()),
        check_vma=False,
    )
```

```python
import functools

import jax
import jax.numpy as jnp
from jax import lax
from jax.experimental import pallas as pl
from jax.experimental.pallas import tpu as pltpu
from jax.sharding import PartitionSpec as P

BF = jnp.bfloat16
F32 = jnp.float32
MESH = pl.DeviceIdType.MESH
COLUMN_PARTS = 1
ROW_TILE = 16


def contract_rows(left, right):
    return lax.dot_general(left, right, (((0,), (0,)), ((), ())), preferred_element_type=F32)


def contract_cols(left, right):
    return lax.dot_general(left, right, (((1,), (1,)), ((), ())), preferred_element_type=F32)


def dot(left, right):
    return jnp.dot(left, right, preferred_element_type=F32)


def round_up(value, step):
    return -(-value // step) * step


def kernel(
    nd, ns,
    features, w_self, w_neigh, cotangent, neighbours, hub_slots, send_rows, send_counts,
    hidden, grad_features, grad_self, grad_neigh,
    pick, picked, hub_out, hub_in, bound_out, bound_in, table, count, agg, zs, dz, eg, accum,
    hub_send, hub_back, bound_send, bound_back, back,
    s1, r1, acc1, s2, r2, acc2, s3, r3, gathered,
    small_send, small_recv, send_sems, recv_sems,
):
    verts, width = features.shape
    slots = neighbours.shape[1]
    devices = nd * ns
    cap = send_rows.shape[2]
    hubs_own = hub_slots.shape[0]
    hub_count = hubs_own * devices
    live_rows = hub_count + ns * cap
    table_size = verts + live_rows
    dom = lax.axis_index("dom")
    shard = lax.axis_index("shard")
    me = dom * ns + shard
    core = lax.rem(dom, 2)
    y = lax.div(dom, 2)
    low = lax.rem(shard, 2)
    high = lax.div(shard, 2)

    def device_of(index):
        return (lax.div(index, ns), lax.rem(index, ns))

    barrier = pltpu.get_barrier_semaphore()

    def greet(k, carry):
        pl.semaphore_signal(
            barrier, inc=1, device_id=device_of(lax.rem(me + k, devices)), device_id_type=MESH
        )
        return carry

    lax.fori_loop(1, devices, greet, 0)

    lane = lax.broadcasted_iota(jnp.int32, (1, verts), 1)
    pick[...] = jnp.zeros_like(pick)
    for p in range(ns):
        for k in range(cap):
            row = jnp.where(k < send_counts[0, p], send_rows[0, p, k], -1)
            pick[pl.ds(p * cap + k, 1), :] = (lane == row).astype(F32)
    for h in range(hubs_own):
        pick[pl.ds(ns * cap + h, 1), :] = (lane == hub_slots[h]).astype(F32)
    picked[...] = dot(pick[...].astype(BF), features[...])
    for p in range(ns):
        bound_out[p] = picked[pl.ds(p * cap, cap), :]
    hub_out[...] = picked[pl.ds(ns * cap, hubs_own), :]

    pl.semaphore_wait(barrier, devices - 1)

    def hub_copy(k):
        return pltpu.make_async_remote_copy(
            src_ref=hub_out,
            dst_ref=hub_in.at[k - 1],
            send_sem=small_send.at[0],
            recv_sem=small_recv.at[0],
            device_id=device_of(lax.rem(me + k, devices)),
            device_id_type=MESH,
        )

    def hub_return(k):
        target = lax.rem(me + k, devices)
        return pltpu.make_async_remote_copy(
            src_ref=hub_send.at[target],
            dst_ref=hub_back.at[k - 1],
            send_sem=small_send.at[1],
            recv_sem=small_recv.at[1],
            device_id=device_of(target),
            device_id_type=MESH,
        )

    def bound_copy(source, landing, number):
        def make(k):
            target = lax.rem(shard + k, ns)
            return pltpu.make_async_remote_copy(
                src_ref=source.at[target],
                dst_ref=landing.at[k - 1],
                send_sem=small_send.at[number],
                recv_sem=small_recv.at[number],
                device_id=(dom, target),
                device_id_type=MESH,
            )

        return make

    def start_all(make, total):
        def one(k, carry):
            make(k).start()
            return carry

        lax.fori_loop(1, total, one, 0)

    def wait_all(landing, number):
        pltpu.make_async_copy(landing, landing, small_recv.at[number]).wait()
        pltpu.make_async_copy(landing, landing, small_send.at[number]).wait()

    start_all(bound_copy(bound_out, bound_in, 2), ns)
    start_all(hub_copy, devices)

    block = 32
    columns = count.shape[1]
    names = lax.broadcasted_iota(jnp.int32, (block, columns), 1)

    def count_block(i, carry):
        rows = pl.ds(pl.multiple_of(i * block, block), block)
        slot = neighbours[rows, :]
        total = jnp.zeros((block, columns), F32)
        for j in range(slots):
            total = total + (slot[:, j : j + 1] == names).astype(F32)
        count[rows, :] = total.astype(BF)
        return carry

    lax.fori_loop(0, verts // block, count_block, 0)
    degree = jnp.sum((neighbours[...] < table_size).astype(F32), axis=1, keepdims=True)
    zs[...] = dot(features[...], w_self[...])
    local_sums = dot(count[:, :verts], features[...])

    table[...] = jnp.zeros_like(table)
    for h in range(hubs_own):
        table[pl.ds(me * hubs_own + h, 1), :] = hub_out[pl.ds(h, 1), :]
    for k in range(cap):
        table[pl.ds(hub_count + shard * cap + k, 1), :] = bound_out[shard, pl.ds(k, 1), :]
    wait_all(bound_in, 2)
    for k in range(1, ns):
        source = lax.rem(shard - k + ns, ns)
        for i in range(cap):
            table[pl.ds(hub_count + source * cap + i, 1), :] = bound_in[k - 1, pl.ds(i, 1), :]
    wait_all(hub_in, 0)

    def place_hub(k, carry):
        source = lax.rem(me - k + devices, devices)
        for h in range(hubs_own):
            table[pl.ds(source * hubs_own + h, 1), :] = hub_in[k - 1, pl.ds(h, 1), :]
        return carry

    lax.fori_loop(1, devices, place_hub, 0)

    sums = local_sums + dot(count[:, verts:], table[...].astype(BF))
    agg[...] = (sums / degree).astype(BF)
    z = zs[...] + dot(agg[...], w_neigh[...])
    sig = jax.nn.sigmoid(z)
    hidden[...] = (z * sig).astype(BF)
    dz[...] = (cotangent[...].astype(F32) * sig * (1.0 + z * (1.0 - sig))).astype(BF)

    part = width // COLUMN_PARTS
    pieces = 2 * COLUMN_PARTS
    plane = (nd // 2) * 2
    tall = ns // 2
    half = width // 2
    rows2 = half // plane
    scatter = rows2 % (tall * ROW_TILE) == 0
    rows3 = rows2 // tall if scatter else rows2
    my_plane = y * 2 + low
    base1 = core * half
    base2 = base1 + my_plane * rows2
    base3 = base2 + high * rows3 if scatter else base2

    def at_core(j):
        return (y * 2 + j, shard)

    def at_plane(j):
        return (lax.div(j, 2) * 2 + core, high * 2 + lax.rem(j, 2))

    def at_tall(j):
        return (dom, j * 2 + low)

    def copy(q, stage, k, source, landing, target):
        return pltpu.make_async_remote_copy(
            src_ref=source,
            dst_ref=landing,
            send_sem=send_sems.at[q, stage, k - 1],
            recv_sem=recv_sems.at[q, stage, k - 1],
            device_id=target,
            device_id_type=MESH,
        )

    def rows_at(start, size):
        return pl.ds(pl.multiple_of(start, ROW_TILE), size)

    def left_of(q):
        return features if q // COLUMN_PARTS == 0 else agg

    def right_of(q):
        return dz[:, pl.ds((q % COLUMN_PARTS) * part, part)]

    def stage0(q):
        other = pl.ds(pl.multiple_of((1 - core) * half, half), half)
        own = pl.ds(pl.multiple_of(core * half, half), half)
        s1[q] = contract_rows(left_of(q)[:, other], right_of(q)).astype(BF)
        c = copy(q, 0, 1, s1.at[q], r1.at[q], at_core(1 - core))
        c.start()
        acc1[q] = contract_rows(left_of(q)[:, own], right_of(q))
        return [c]

    def stage1(q):
        acc1[q] = acc1[q] + r1[q].astype(F32)
        copies = []
        for k in range(1, plane):
            j = lax.rem(my_plane + k, plane)
            s2[q, k - 1] = acc1[q, rows_at(j * rows2, rows2), :].astype(BF)
            c = copy(q, 1, k, s2.at[q, k - 1], r2.at[q, k - 1], at_plane(j))
            c.start()
            copies.append(c)
        return copies

    def stage2(q):
        total = acc1[q, rows_at(my_plane * rows2, rows2), :]
        for k in range(1, plane):
            total = total + r2[q, k - 1].astype(F32)
        acc2[q] = total
        copies = []
        if not scatter:
            r3[q, high] = total.astype(BF)
        for k in range(1, tall):
            j = lax.rem(high + k, tall)
            if scatter:
                s3[q, k - 1] = acc2[q, rows_at(j * rows3, rows3), :].astype(BF)
                c = copy(q, 2, k, s3.at[q, k - 1], r3.at[q, k - 1], at_tall(j))
            else:
                c = copy(q, 2, k, r3.at[q, high], r3.at[q, high], at_tall(j))
            c.start()
            copies.append(c)
        return copies

    def stage3(q):
        if scatter:
            total = acc2[q, rows_at(high * rows3, rows3), :]
            for k in range(1, tall):
                total = total + r3[q, k - 1].astype(F32)
        else:
            total = r3[q, 0].astype(F32)
            for j in range(1, tall):
                total = total + r3[q, j].astype(F32)
        gathered[q, rows_at(base3, rows3), :] = total.astype(BF)
        copies = []
        if scatter:
            chunk = gathered.at[q, rows_at(base3, rows3), :]
            for k in range(1, tall):
                c = copy(q, 3, k, chunk, chunk, at_tall(lax.rem(high + k, tall)))
                c.start()
                copies.append(c)
        return copies

    def stage4(q):
        chunk = gathered.at[q, rows_at(base2, rows2), :]
        copies = []
        for k in range(1, plane):
            c = copy(q, 4, k, chunk, chunk, at_plane(lax.rem(my_plane + k, plane)))
            c.start()
            copies.append(c)
        return copies

    def stage5(q):
        chunk = gathered.at[q, rows_at(base1, half), :]
        c = copy(q, 5, 1, chunk, chunk, at_core(1 - core))
        c.start()
        return [c]

    def finish(copies):
        for c in copies:
            c.wait()

    stages = [stage0, stage1, stage2, stage3, stage4, stage5]
    flying = [stage0(q) for q in range(pieces)]
    for number in range(1, len(stages)):
        for q in range(pieces):
            finish(flying[q])
            flying[q] = stages[number](q)
            if number == 1 and q == 0:
                eg[...] = (contract_cols(dz[...], w_neigh[...]) / degree).astype(BF)
                accum[...] = contract_rows(count[:, verts:], eg[...])

                def fill(d, carry):
                    for h in range(hubs_own):
                        hub_send[d, pl.ds(h, 1), :] = accum[pl.ds(d * hubs_own + h, 1), :]
                    return carry

                lax.fori_loop(0, devices, fill, 0)
                for p in range(ns):
                    bound_send[p] = accum[pl.ds(hub_count + p * cap, cap), :]
                start_all(bound_copy(bound_send, bound_back, 3), ns)
                start_all(hub_return, devices)
            if number == 2 and q == 0:
                grad_features[...] = contract_cols(dz[...], w_self[...]) + contract_rows(
                    count[:, :verts], eg[...]
                )
            if number == 4 and q == pieces - 1:
                back[...] = jnp.zeros_like(back)
                for i in range(cap):
                    back[pl.ds(shard * cap + i, 1), :] = bound_send[shard, pl.ds(i, 1), :]
                wait_all(bound_back, 3)
                for k in range(1, ns):
                    source = lax.rem(shard - k + ns, ns)
                    for i in range(cap):
                        back[pl.ds(source * cap + i, 1), :] = bound_back[k - 1, pl.ds(i, 1), :]
                wait_all(hub_back, 1)
                back[pl.ds(ns * cap, hubs_own), :] = hub_send[me] + jnp.sum(hub_back[...], axis=0)
                grad_features[...] = grad_features[...] + contract_rows(
                    pick[...].astype(BF), back[...].astype(BF)
                )
    for q in range(pieces):
        finish(flying[q])
        out = grad_self if q // COLUMN_PARTS == 0 else grad_neigh
        out[:, pl.ds((q % COLUMN_PARTS) * part, part)] = gathered[q].astype(F32)


def body(nd, ns, features, w_self, w_neigh, cotangent, neighbours, hub_slots, send_rows, send_counts):
    verts, width = features.shape
    cap = send_rows.shape[2]
    hubs_own = hub_slots.shape[0]
    devices = nd * ns
    extra = round_up(hubs_own * devices + ns * cap, 128)
    picks = round_up(ns * cap + hubs_own, 16)
    pieces = 2 * COLUMN_PARTS
    part = width // COLUMN_PARTS
    plane = (nd // 2) * 2
    tall = ns // 2
    half = width // 2
    rows2 = half // plane
    scatter = rows2 % (tall * ROW_TILE) == 0
    rows3 = rows2 // tall if scatter else rows2
    landings = tall - 1 if scatter else tall
    most = max(plane, tall) - 1
    vmem = pl.BlockSpec(memory_space=pltpu.VMEM)
    smem = pl.BlockSpec(memory_space=pltpu.SMEM)
    return pl.pallas_call(
        functools.partial(kernel, nd, ns),
        out_shape=(
            jax.ShapeDtypeStruct((verts, width), BF),
            jax.ShapeDtypeStruct((verts, width), F32),
            jax.ShapeDtypeStruct((width, width), F32),
            jax.ShapeDtypeStruct((width, width), F32),
        ),
        in_specs=[vmem] * 5 + [smem] * 3,
        out_specs=[vmem] * 4,
        scratch_shapes=[
            pltpu.VMEM((picks, verts), F32),
            pltpu.VMEM((picks, width), F32),
            pltpu.VMEM((hubs_own, width), F32),
            pltpu.VMEM((devices - 1, hubs_own, width), F32),
            pltpu.VMEM((ns, cap, width), F32),
            pltpu.VMEM((ns - 1, cap, width), F32),
            pltpu.VMEM((extra, width), F32),
            pltpu.VMEM((verts, verts + extra), BF),
            pltpu.VMEM((verts, width), BF),
            pltpu.VMEM((verts, width), F32),
            pltpu.VMEM((verts, width), BF),
            pltpu.VMEM((verts, width), BF),
            pltpu.VMEM((extra, width), F32),
            pltpu.VMEM((devices, hubs_own, width), F32),
            pltpu.VMEM((devices - 1, hubs_own, width), F32),
            pltpu.VMEM((ns, cap, width), F32),
            pltpu.VMEM((ns - 1, cap, width), F32),
            pltpu.VMEM((picks, width), F32),
            pltpu.VMEM((pieces, half, part), BF),
            pltpu.VMEM((pieces, half, part), BF),
            pltpu.VMEM((pieces, half, part), F32),
            pltpu.VMEM((pieces, plane - 1, rows2, part), BF),
            pltpu.VMEM((pieces, plane - 1, rows2, part), BF),
            pltpu.VMEM((pieces, rows2, part), F32),
            pltpu.VMEM((pieces, tall - 1, rows3, part), BF),
            pltpu.VMEM((pieces, landings, rows3, part), BF),
            pltpu.VMEM((pieces, width, part), BF),
            pltpu.SemaphoreType.DMA((4,)),
            pltpu.SemaphoreType.DMA((4,)),
            pltpu.SemaphoreType.DMA((pieces, 6, most)),
            pltpu.SemaphoreType.DMA((pieces, 6, most)),
        ],
        compiler_params=pltpu.CompilerParams(
            collective_id=0, has_side_effects=True, vmem_limit_bytes=40 * 1024 * 1024
        ),
    )(features, w_self, w_neigh, cotangent, neighbours, hub_slots, send_rows, send_counts)


def solution(mesh):
    both = ("dom", "shard")
    return jax.shard_map(
        functools.partial(body, mesh.shape["dom"], mesh.shape["shard"]),
        mesh=mesh,
        in_specs=(
            P(both, None),
            P(),
            P(),
            P(both, None),
            P(both, None),
            P(both),
            P(both, None, None),
            P(both, None),
        ),
        out_specs=(P(both, None), P(both, None), P(), P()),
        check_vma=False,
    )
```

```python
import functools

import jax
import jax.numpy as jnp
from jax import lax
from jax.experimental import pallas as pl
from jax.experimental.pallas import tpu as pltpu
from jax.sharding import PartitionSpec as P

BF = jnp.bfloat16
F32 = jnp.float32
MESH = pl.DeviceIdType.MESH
COLUMN_PARTS = 1
ROW_TILE = 16
VMEM_GRANT = 60 * 1024 * 1024


def contract_rows(left, right):
    return lax.dot_general(left, right, (((0,), (0,)), ((), ())), preferred_element_type=F32)


def contract_cols(left, right):
    return lax.dot_general(left, right, (((1,), (1,)), ((), ())), preferred_element_type=F32)


def dot(left, right):
    return jnp.dot(left, right, preferred_element_type=F32)


def round_up(value, step):
    return -(-value // step) * step


def kernel(
    nd, ns,
    features_hbm, w_self_hbm, w_neigh_hbm, cotangent_hbm, neighbours_hbm, rows_hbm, counts_hbm,
    hub_slots,
    hidden_hbm, grad_features_hbm, gathered_hbm,
    hidden, grad_features, store_sems,
    features, w_self, w_neigh, cotangent, neighbours, send_rows, send_counts, load_sems,
    pick, picked, hub_out, hub_in, bound_out, bound_in, table, count, agg, zs, dz, eg, accum,
    hub_send, hub_back, bound_send, bound_back, back,
    s1, r1, acc1, s2, r2, acc2, s3, r3, gathered,
    small_send, small_recv, send_sems, recv_sems,
):
    verts, width = features.shape
    slots = neighbours.shape[0]
    devices = nd * ns
    cap = send_rows.shape[1]
    hubs_own = hub_slots.shape[0]
    hub_count = hubs_own * devices
    live_rows = hub_count + ns * cap
    table_size = verts + live_rows
    dom = lax.axis_index("dom")
    shard = lax.axis_index("shard")
    me = dom * ns + shard
    core = lax.rem(dom, 2)
    y = lax.div(dom, 2)
    low = lax.rem(shard, 2)
    high = lax.div(shard, 2)

    def device_of(index):
        return (lax.div(index, ns), lax.rem(index, ns))

    pairs = (
        (rows_hbm, send_rows),
        (counts_hbm, send_counts),
        (features_hbm, features),
        (neighbours_hbm, neighbours),
        (w_self_hbm, w_self),
        (w_neigh_hbm, w_neigh),
        (cotangent_hbm, cotangent),
    )
    loads = [pltpu.make_async_copy(a, b, load_sems.at[i]) for i, (a, b) in enumerate(pairs)]
    for load in loads:
        load.start()

    barrier = pltpu.get_barrier_semaphore()

    def greet(k, carry):
        pl.semaphore_signal(
            barrier, inc=1, device_id=device_of(lax.rem(me + k, devices)), device_id_type=MESH
        )
        return carry

    lax.fori_loop(1, devices, greet, 0)

    lane = lax.broadcasted_iota(jnp.int32, (1, verts), 1)
    pick[...] = jnp.zeros_like(pick)
    loads[0].wait()
    loads[1].wait()
    for p in range(ns):
        for k in range(cap):
            row = jnp.where(k < send_counts[0, p], send_rows[0, k, p], -1)
            pick[pl.ds(p * cap + k, 1), :] = (lane == row).astype(F32)
    for h in range(hubs_own):
        pick[pl.ds(ns * cap + h, 1), :] = (lane == hub_slots[h]).astype(F32)
    loads[2].wait()
    picked[...] = dot(pick[...].astype(BF), features[...])
    for p in range(ns):
        bound_out[p] = picked[pl.ds(p * cap, cap), :]
    hub_out[...] = picked[pl.ds(ns * cap, hubs_own), :]

    pl.semaphore_wait(barrier, devices - 1)

    def hub_copy(k):
        return pltpu.make_async_remote_copy(
            src_ref=hub_out,
            dst_ref=hub_in.at[k - 1],
            send_sem=small_send.at[0],
            recv_sem=small_recv.at[0],
            device_id=device_of(lax.rem(me + k, devices)),
            device_id_type=MESH,
        )

    def hub_return(k):
        target = lax.rem(me + k, devices)
        return pltpu.make_async_remote_copy(
            src_ref=hub_send.at[target],
            dst_ref=hub_back.at[k - 1],
            send_sem=small_send.at[1],
            recv_sem=small_recv.at[1],
            device_id=device_of(target),
            device_id_type=MESH,
        )

    def bound_copy(source, landing, number):
        def make(k):
            target = lax.rem(shard + k, ns)
            return pltpu.make_async_remote_copy(
                src_ref=source.at[target],
                dst_ref=landing.at[k - 1],
                send_sem=small_send.at[number],
                recv_sem=small_recv.at[number],
                device_id=(dom, target),
                device_id_type=MESH,
            )

        return make

    def start_all(make, total):
        def one(k, carry):
            make(k).start()
            return carry

        lax.fori_loop(1, total, one, 0)

    def wait_all(landing, number):
        pltpu.make_async_copy(landing, landing, small_recv.at[number]).wait()
        pltpu.make_async_copy(landing, landing, small_send.at[number]).wait()

    start_all(bound_copy(bound_out, bound_in, 2), ns)
    start_all(hub_copy, devices)

    block = 64
    names = lax.broadcasted_iota(jnp.int32, (block, verts), 0)
    loads[3].wait()

    def count_block(i, carry):
        first = pl.multiple_of(i * block, block)
        total = jnp.zeros((block, verts), F32)
        for j in range(slots):
            total = total + (neighbours[pl.ds(j, 1), :] - first == names).astype(F32)
        count[pl.ds(first, block), :] = total.astype(BF)
        return carry

    lax.fori_loop(0, count.shape[0] // block, count_block, 0)
    alive = (neighbours[...] < table_size).astype(F32).astype(BF)
    degree = contract_rows(alive, jnp.ones((slots, 128), BF))
    degree = jnp.concatenate([degree] * (width // 128), axis=1)
    loads[4].wait()
    zs[...] = dot(features[...], w_self[...])
    local_sums = contract_rows(count[:verts, :], features[...])

    table[...] = jnp.zeros_like(table)
    for h in range(hubs_own):
        table[pl.ds(me * hubs_own + h, 1), :] = hub_out[pl.ds(h, 1), :]
    for k in range(cap):
        table[pl.ds(hub_count + shard * cap + k, 1), :] = bound_out[shard, pl.ds(k, 1), :]
    wait_all(bound_in, 2)
    for k in range(1, ns):
        source = lax.rem(shard - k + ns, ns)
        for i in range(cap):
            table[pl.ds(hub_count + source * cap + i, 1), :] = bound_in[k - 1, pl.ds(i, 1), :]
    wait_all(hub_in, 0)

    def place_hub(k, carry):
        source = lax.rem(me - k + devices, devices)
        for h in range(hubs_own):
            table[pl.ds(source * hubs_own + h, 1), :] = hub_in[k - 1, pl.ds(h, 1), :]
        return carry

    lax.fori_loop(1, devices, place_hub, 0)

    loads[5].wait()
    loads[6].wait()
    sums = local_sums + contract_rows(count[verts:, :], table[...].astype(BF))
    agg[...] = (sums / degree).astype(BF)
    z = zs[...] + dot(agg[...], w_neigh[...])
    sig = jax.nn.sigmoid(z)
    hidden[...] = (z * sig).astype(BF)
    stores = [pltpu.make_async_copy(hidden, hidden_hbm, store_sems.at[0])]
    stores[0].start()
    dz[...] = (cotangent[...].astype(F32) * sig * (1.0 + z * (1.0 - sig))).astype(BF)

    part = width // COLUMN_PARTS
    pieces = 2 * COLUMN_PARTS
    plane = (nd // 2) * 2
    tall = ns // 2
    half = width // 2
    rows2 = half // plane
    scatter = rows2 % (tall * ROW_TILE) == 0
    rows3 = rows2 // tall if scatter else rows2
    my_plane = y * 2 + low
    base1 = core * half
    base2 = base1 + my_plane * rows2
    base3 = base2 + high * rows3 if scatter else base2

    def at_core(j):
        return (y * 2 + j, shard)

    def at_plane(j):
        return (lax.div(j, 2) * 2 + core, high * 2 + lax.rem(j, 2))

    def at_tall(j):
        return (dom, j * 2 + low)

    def copy(q, stage, k, source, landing, target):
        return pltpu.make_async_remote_copy(
            src_ref=source,
            dst_ref=landing,
            send_sem=send_sems.at[q, stage, k - 1],
            recv_sem=recv_sems.at[q, stage, k - 1],
            device_id=target,
            device_id_type=MESH,
        )

    def rows_at(start, size):
        return pl.ds(pl.multiple_of(start, ROW_TILE), size)

    def left_of(q):
        return features if q // COLUMN_PARTS == 0 else agg

    def right_of(q):
        return dz[:, pl.ds((q % COLUMN_PARTS) * part, part)]

    def stage0(q):
        other = pl.ds(pl.multiple_of((1 - core) * half, half), half)
        own = pl.ds(pl.multiple_of(core * half, half), half)
        s1[q] = contract_rows(left_of(q)[:, other], right_of(q)).astype(BF)
        c = copy(q, 0, 1, s1.at[q], r1.at[q], at_core(1 - core))
        c.start()
        acc1[q] = contract_rows(left_of(q)[:, own], right_of(q))
        return [c]

    def stage1(q):
        acc1[q] = acc1[q] + r1[q].astype(F32)
        copies = []
        for k in range(1, plane):
            j = lax.rem(my_plane + k, plane)
            s2[q, k - 1] = acc1[q, rows_at(j * rows2, rows2), :].astype(BF)
            c = copy(q, 1, k, s2.at[q, k - 1], r2.at[q, k - 1], at_plane(j))
            c.start()
            copies.append(c)
        return copies

    def stage2(q):
        total = acc1[q, rows_at(my_plane * rows2, rows2), :]
        for k in range(1, plane):
            total = total + r2[q, k - 1].astype(F32)
        acc2[q] = total
        copies = []
        if not scatter:
            r3[q, high] = total.astype(BF)
        for k in range(1, tall):
            j = lax.rem(high + k, tall)
            if scatter:
                s3[q, k - 1] = acc2[q, rows_at(j * rows3, rows3), :].astype(BF)
                c = copy(q, 2, k, s3.at[q, k - 1], r3.at[q, k - 1], at_tall(j))
            else:
                c = copy(q, 2, k, r3.at[q, high], r3.at[q, high], at_tall(j))
            c.start()
            copies.append(c)
        return copies

    def stage3(q):
        if scatter:
            total = acc2[q, rows_at(high * rows3, rows3), :]
            for k in range(1, tall):
                total = total + r3[q, k - 1].astype(F32)
        else:
            total = r3[q, 0].astype(F32)
            for j in range(1, tall):
                total = total + r3[q, j].astype(F32)
        gathered[q, rows_at(base3, rows3), :] = total.astype(BF)
        copies = []
        if scatter:
            chunk = gathered.at[q, rows_at(base3, rows3), :]
            for k in range(1, tall):
                c = copy(q, 3, k, chunk, chunk, at_tall(lax.rem(high + k, tall)))
                c.start()
                copies.append(c)
        return copies

    def stage4(q):
        chunk = gathered.at[q, rows_at(base2, rows2), :]
        copies = []
        for k in range(1, plane):
            c = copy(q, 4, k, chunk, chunk, at_plane(lax.rem(my_plane + k, plane)))
            c.start()
            copies.append(c)
        return copies

    def stage5(q):
        chunk = gathered.at[q, rows_at(base1, half), :]
        c = copy(q, 5, 1, chunk, chunk, at_core(1 - core))
        c.start()
        return [c]

    def finish(copies):
        for c in copies:
            c.wait()

    stages = [stage0, stage1, stage2, stage3, stage4, stage5]
    flying = [stage0(q) for q in range(pieces)]
    for number in range(1, len(stages)):
        for q in range(pieces):
            finish(flying[q])
            flying[q] = stages[number](q)
            if number == 1 and q == 0:
                eg[...] = (contract_cols(dz[...], w_neigh[...]) / degree).astype(BF)
                accum[...] = dot(count[verts:, :], eg[...])

                def fill(d, carry):
                    for h in range(hubs_own):
                        hub_send[d, pl.ds(h, 1), :] = accum[pl.ds(d * hubs_own + h, 1), :]
                    return carry

                lax.fori_loop(0, devices, fill, 0)
                for p in range(ns):
                    bound_send[p] = accum[pl.ds(hub_count + p * cap, cap), :]
                start_all(bound_copy(bound_send, bound_back, 3), ns)
                start_all(hub_return, devices)
            if number == 2 and q == 0:
                grad_features[...] = contract_cols(dz[...], w_self[...]) + dot(
                    count[:verts, :], eg[...]
                )
            if number == 4 and q == pieces - 1:
                back[...] = jnp.zeros_like(back)
                for i in range(cap):
                    back[pl.ds(shard * cap + i, 1), :] = bound_send[shard, pl.ds(i, 1), :]
                wait_all(bound_back, 3)
                for k in range(1, ns):
                    source = lax.rem(shard - k + ns, ns)
                    for i in range(cap):
                        back[pl.ds(source * cap + i, 1), :] = bound_back[k - 1, pl.ds(i, 1), :]
                wait_all(hub_back, 1)
                back[pl.ds(ns * cap, hubs_own), :] = hub_send[me] + jnp.sum(hub_back[...], axis=0)
                grad_features[...] = grad_features[...] + contract_rows(
                    pick[...].astype(BF), back[...].astype(BF)
                )
                stores.append(
                    pltpu.make_async_copy(grad_features, grad_features_hbm, store_sems.at[1])
                )
                stores[-1].start()
    for q in range(pieces):
        finish(flying[q])
        stores.append(
            pltpu.make_async_copy(gathered.at[q], gathered_hbm.at[q], store_sems.at[2 + q])
        )
        stores[-1].start()
    for store in stores:
        store.wait()


def writer(
    hidden_in, grad_features_in, gathered_in, hidden, grad_features, grad_self, grad_neigh,
    narrow, wide, in_sems, out_sems,
):
    pieces, width, part = narrow.shape
    cuts = in_sems.shape[1]
    step = width // cuts
    places = [(q, i) for q in range(pieces) for i in range(cuts)]
    reads = []
    for q, i in places:
        rows = pl.ds(i * step, step)
        reads.append(
            pltpu.make_async_copy(gathered_in.at[q, rows], narrow.at[q, rows], in_sems.at[q, i])
        )
        reads[-1].start()
    writes = [
        pltpu.make_async_copy(hidden_in, hidden, out_sems.at[pieces, 0]),
        pltpu.make_async_copy(grad_features_in, grad_features, out_sems.at[pieces, 1]),
    ]
    for c in writes:
        c.start()
    for read, (q, i) in zip(reads, places):
        read.wait()
        rows = pl.ds(i * step, step)
        cols = pl.ds((q % COLUMN_PARTS) * part, part)
        wide[q, rows, :] = narrow[q, rows, :].astype(F32)
        out = grad_self if q // COLUMN_PARTS == 0 else grad_neigh
        writes.append(
            pltpu.make_async_copy(wide.at[q, rows], out.at[rows, cols], out_sems.at[q, i])
        )
        writes[-1].start()
    for c in writes:
        c.wait()


def body(nd, ns, features, w_self, w_neigh, cotangent, neighbours, hub_slots, send_rows, send_counts):
    verts, width = features.shape
    cap = send_rows.shape[2]
    hubs_own = hub_slots.shape[0]
    devices = nd * ns
    extra = round_up(hubs_own * devices + ns * cap, 128)
    picks = round_up(ns * cap + hubs_own, 16)
    pieces = 2 * COLUMN_PARTS
    part = width // COLUMN_PARTS
    plane = (nd // 2) * 2
    tall = ns // 2
    half = width // 2
    rows2 = half // plane
    scatter = rows2 % (tall * ROW_TILE) == 0
    rows3 = rows2 // tall if scatter else rows2
    landings = tall - 1 if scatter else tall
    most = max(plane, tall) - 1
    smem = pl.BlockSpec(memory_space=pltpu.SMEM)
    hbm = pl.BlockSpec(memory_space=pltpu.HBM)
    shapes = (
        jax.ShapeDtypeStruct((verts, width), BF),
        jax.ShapeDtypeStruct((verts, width), F32),
        jax.ShapeDtypeStruct((width, width), F32),
        jax.ShapeDtypeStruct((width, width), F32),
    )
    results = pl.pallas_call(
        functools.partial(kernel, nd, ns),
        out_shape=shapes[:2] + (jax.ShapeDtypeStruct((pieces, width, part), BF),),
        in_specs=[hbm] * 7 + [smem],
        out_specs=[hbm] * 3,
        scratch_shapes=[
            pltpu.VMEM((verts, width), BF),
            pltpu.VMEM((verts, width), F32),
            pltpu.SemaphoreType.DMA((2 + pieces,)),
            pltpu.VMEM((verts, width), BF),
            pltpu.VMEM((width, width), BF),
            pltpu.VMEM((width, width), BF),
            pltpu.VMEM((verts, width), BF),
            pltpu.VMEM((neighbours.shape[1], verts), jnp.int32),
            pltpu.SMEM((1, cap, ns), jnp.int32),
            pltpu.SMEM((1, ns), jnp.int32),
            pltpu.SemaphoreType.DMA((7,)),
            pltpu.VMEM((picks, verts), F32),
            pltpu.VMEM((picks, width), F32),
            pltpu.VMEM((hubs_own, width), F32),
            pltpu.VMEM((devices - 1, hubs_own, width), F32),
            pltpu.VMEM((ns, cap, width), F32),
            pltpu.VMEM((ns - 1, cap, width), F32),
            pltpu.VMEM((extra, width), F32),
            pltpu.VMEM((verts + extra, verts), BF),
            pltpu.VMEM((verts, width), BF),
            pltpu.VMEM((verts, width), F32),
            pltpu.VMEM((verts, width), BF),
            pltpu.VMEM((verts, width), BF),
            pltpu.VMEM((extra, width), F32),
            pltpu.VMEM((devices, hubs_own, width), F32),
            pltpu.VMEM((devices - 1, hubs_own, width), F32),
            pltpu.VMEM((ns, cap, width), F32),
            pltpu.VMEM((ns - 1, cap, width), F32),
            pltpu.VMEM((picks, width), F32),
            pltpu.VMEM((pieces, half, part), BF),
            pltpu.VMEM((pieces, half, part), BF),
            pltpu.VMEM((pieces, half, part), F32),
            pltpu.VMEM((pieces, plane - 1, rows2, part), BF),
            pltpu.VMEM((pieces, plane - 1, rows2, part), BF),
            pltpu.VMEM((pieces, rows2, part), F32),
            pltpu.VMEM((pieces, tall - 1, rows3, part), BF),
            pltpu.VMEM((pieces, landings, rows3, part), BF),
            pltpu.VMEM((pieces, width, part), BF),
            pltpu.SemaphoreType.DMA((4,)),
            pltpu.SemaphoreType.DMA((4,)),
            pltpu.SemaphoreType.DMA((pieces, 6, most)),
            pltpu.SemaphoreType.DMA((pieces, 6, most)),
        ],
        compiler_params=pltpu.CompilerParams(
            collective_id=0, has_side_effects=True, vmem_limit_bytes=VMEM_GRANT
        ),
    )(
        features, w_self, w_neigh, cotangent, neighbours.T, send_rows.transpose(0, 2, 1),
        send_counts, hub_slots,
    )
    return pl.pallas_call(
        writer,
        out_shape=shapes,
        in_specs=[hbm] * 3,
        out_specs=[hbm] * 4,
        scratch_shapes=[
            pltpu.VMEM((pieces, width, part), BF),
            pltpu.VMEM((pieces, width, part), F32),
            pltpu.SemaphoreType.DMA((pieces, 2)),
            pltpu.SemaphoreType.DMA((pieces + 1, 2)),
        ],
        compiler_params=pltpu.CompilerParams(vmem_limit_bytes=VMEM_GRANT),
    )(*results)


def solution(mesh):
    both = ("dom", "shard")
    return jax.shard_map(
        functools.partial(body, mesh.shape["dom"], mesh.shape["shard"]),
        mesh=mesh,
        in_specs=(
            P(both, None),
            P(),
            P(),
            P(both, None),
            P(both, None),
            P(both),
            P(both, None, None),
            P(both, None),
        ),
        out_specs=(P(both, None), P(both, None), P(), P()),
        check_vma=False,
    )
```

```python
import functools

import jax
import jax.numpy as jnp
from jax import lax
from jax.experimental import pallas as pl
from jax.experimental.pallas import tpu as pltpu
from jax.sharding import PartitionSpec as P

BF = jnp.bfloat16
F32 = jnp.float32
MESH = pl.DeviceIdType.MESH
COLUMN_PARTS = 1
ROW_TILE = 16
VMEM_GRANT = 60 * 1024 * 1024


def contract_rows(left, right):
    return lax.dot_general(left, right, (((0,), (0,)), ((), ())), preferred_element_type=F32)


def contract_cols(left, right):
    return lax.dot_general(left, right, (((1,), (1,)), ((), ())), preferred_element_type=F32)


def dot(left, right):
    return jnp.dot(left, right, preferred_element_type=F32)


def round_up(value, step):
    return -(-value // step) * step


def kernel(
    nd, ns,
    features_hbm, w_self_hbm, w_neigh_hbm, cotangent_hbm, neighbours_hbm, rows_hbm, counts_hbm,
    hub_slots,
    hidden_hbm, grad_features_hbm, gathered_hbm,
    hidden, grad_features, store_sems,
    features, w_self, w_neigh, cotangent, neighbours, send_rows, send_counts, load_sems,
    pick, picked, hub_out, hub_in, bound_out, bound_in, table, count, agg, zs, dz, eg, accum,
    hub_send, hub_back, bound_send, bound_back, back,
    s1, r1, acc1, s2, r2, acc2, s3, r3, gathered,
    small_send, small_recv, send_sems, recv_sems,
):
    verts, width = features.shape
    slots = neighbours.shape[0]
    devices = nd * ns
    cap = send_rows.shape[1]
    hubs_own = hub_slots.shape[0]
    hub_count = hubs_own * devices
    live_rows = hub_count + ns * cap
    table_size = verts + live_rows
    dom = lax.axis_index("dom")
    shard = lax.axis_index("shard")
    me = dom * ns + shard
    core = lax.rem(dom, 2)
    y = lax.div(dom, 2)
    low = lax.rem(shard, 2)
    high = lax.div(shard, 2)

    def device_of(index):
        return (lax.div(index, ns), lax.rem(index, ns))

    pairs = (
        (rows_hbm, send_rows),
        (counts_hbm, send_counts),
        (features_hbm, features),
        (neighbours_hbm, neighbours),
        (w_self_hbm, w_self),
        (w_neigh_hbm, w_neigh),
        (cotangent_hbm, cotangent),
    )
    loads = [pltpu.make_async_copy(a, b, load_sems.at[i]) for i, (a, b) in enumerate(pairs)]
    for load in loads:
        load.start()

    barrier = pltpu.get_barrier_semaphore()

    def greet(k, carry):
        pl.semaphore_signal(
            barrier, inc=1, device_id=device_of(lax.rem(me + k, devices)), device_id_type=MESH
        )
        return carry

    lax.fori_loop(1, devices, greet, 0)

    lane = lax.broadcasted_iota(jnp.int32, (1, verts), 1)
    pick[...] = jnp.zeros_like(pick)
    loads[0].wait()
    loads[1].wait()
    for p in range(ns):
        for k in range(cap):
            row = jnp.where(k < send_counts[0, p], send_rows[0, k, p], -1)
            pick[pl.ds(p * cap + k, 1), :] = (lane == row).astype(F32)
    for h in range(hubs_own):
        pick[pl.ds(ns * cap + h, 1), :] = (lane == hub_slots[h]).astype(F32)
    loads[2].wait()
    picked[...] = dot(pick[...].astype(BF), features[...])
    for p in range(ns):
        bound_out[p] = picked[pl.ds(p * cap, cap), :]
    hub_out[...] = picked[pl.ds(ns * cap, hubs_own), :]

    pl.semaphore_wait(barrier, devices - 1)

    def hub_copy(k):
        return pltpu.make_async_remote_copy(
            src_ref=hub_out,
            dst_ref=hub_in.at[k - 1],
            send_sem=small_send.at[0],
            recv_sem=small_recv.at[0],
            device_id=device_of(lax.rem(me + k, devices)),
            device_id_type=MESH,
        )

    def hub_return(k):
        target = lax.rem(me + k, devices)
        return pltpu.make_async_remote_copy(
            src_ref=hub_send.at[target],
            dst_ref=hub_back.at[k - 1],
            send_sem=small_send.at[1],
            recv_sem=small_recv.at[1],
            device_id=device_of(target),
            device_id_type=MESH,
        )

    def bound_copy(source, landing, number):
        def make(k):
            target = lax.rem(shard + k, ns)
            return pltpu.make_async_remote_copy(
                src_ref=source.at[target],
                dst_ref=landing.at[k - 1],
                send_sem=small_send.at[number],
                recv_sem=small_recv.at[number],
                device_id=(dom, target),
                device_id_type=MESH,
            )

        return make

    def start_all(make, total):
        def one(k, carry):
            make(k).start()
            return carry

        lax.fori_loop(1, total, one, 0)

    def wait_all(landing, number):
        pltpu.make_async_copy(landing, landing, small_recv.at[number]).wait()
        pltpu.make_async_copy(landing, landing, small_send.at[number]).wait()

    start_all(bound_copy(bound_out, bound_in, 2), ns)
    start_all(hub_copy, devices)

    block = 64
    names = lax.broadcasted_iota(jnp.int32, (block, verts), 0)
    loads[3].wait()

    def count_block(i, carry):
        first = pl.multiple_of(i * block, block)
        total = jnp.zeros((block, verts), F32)
        for j in range(slots):
            total = total + (neighbours[pl.ds(j, 1), :] - first == names).astype(F32)
        count[pl.ds(first, block), :] = total.astype(BF)
        return carry

    lax.fori_loop(0, count.shape[0] // block, count_block, 0)
    alive = (neighbours[...] < table_size).astype(F32).astype(BF)
    degree = contract_rows(alive, jnp.ones((slots, 128), BF))
    degree = jnp.concatenate([degree] * (width // 128), axis=1)
    loads[4].wait()
    zs[...] = dot(features[...], w_self[...])
    local_sums = contract_rows(count[:verts, :], features[...])

    table[...] = jnp.zeros_like(table)
    for h in range(hubs_own):
        table[pl.ds(me * hubs_own + h, 1), :] = hub_out[pl.ds(h, 1), :]
    for k in range(cap):
        table[pl.ds(hub_count + shard * cap + k, 1), :] = bound_out[shard, pl.ds(k, 1), :]
    wait_all(bound_in, 2)
    for k in range(1, ns):
        source = lax.rem(shard - k + ns, ns)
        for i in range(cap):
            table[pl.ds(hub_count + source * cap + i, 1), :] = bound_in[k - 1, pl.ds(i, 1), :]
    wait_all(hub_in, 0)

    def place_hub(k, carry):
        source = lax.rem(me - k + devices, devices)
        for h in range(hubs_own):
            table[pl.ds(source * hubs_own + h, 1), :] = hub_in[k - 1, pl.ds(h, 1), :]
        return carry

    lax.fori_loop(1, devices, place_hub, 0)

    loads[5].wait()
    loads[6].wait()
    sums = local_sums + contract_rows(count[verts:, :], table[...].astype(BF))
    agg[...] = (sums / degree).astype(BF)
    z = zs[...] + dot(agg[...], w_neigh[...])
    sig = jax.nn.sigmoid(z)
    hidden[...] = (z * sig).astype(BF)
    stores = [pltpu.make_async_copy(hidden, hidden_hbm, store_sems.at[0])]
    stores[0].start()
    dz[...] = (cotangent[...].astype(F32) * sig * (1.0 + z * (1.0 - sig))).astype(BF)

    part = width // COLUMN_PARTS
    pieces = 2 * COLUMN_PARTS
    plane = (nd // 2) * 2
    tall = ns // 2
    half = width // 2
    rows2 = half // plane
    scatter = rows2 % (tall * ROW_TILE) == 0
    rows3 = rows2 // tall if scatter else rows2
    my_plane = y * 2 + low
    base1 = core * half
    base2 = base1 + my_plane * rows2
    base3 = base2 + high * rows3 if scatter else base2

    def at_core(j):
        return (y * 2 + j, shard)

    def at_plane(j):
        return (lax.div(j, 2) * 2 + core, high * 2 + lax.rem(j, 2))

    def at_tall(j):
        return (dom, j * 2 + low)

    def copy(q, stage, k, source, landing, target):
        return pltpu.make_async_remote_copy(
            src_ref=source,
            dst_ref=landing,
            send_sem=send_sems.at[q, stage, k - 1],
            recv_sem=recv_sems.at[q, stage, k - 1],
            device_id=target,
            device_id_type=MESH,
        )

    def rows_at(start, size):
        return pl.ds(pl.multiple_of(start, ROW_TILE), size)

    def left_of(q):
        return features if q // COLUMN_PARTS == 0 else agg

    def right_of(q):
        return dz[:, pl.ds((q % COLUMN_PARTS) * part, part)]

    def stage0(q):
        other = pl.ds(pl.multiple_of((1 - core) * half, half), half)
        own = pl.ds(pl.multiple_of(core * half, half), half)
        s1[q] = contract_rows(left_of(q)[:, other], right_of(q)).astype(BF)
        c = copy(q, 0, 1, s1.at[q], r1.at[q], at_core(1 - core))
        c.start()
        acc1[q] = contract_rows(left_of(q)[:, own], right_of(q))
        return [c]

    def stage1(q):
        acc1[q] = acc1[q] + r1[q].astype(F32)
        copies = []
        for k in range(1, plane):
            j = lax.rem(my_plane + k, plane)
            s2[q, k - 1] = acc1[q, rows_at(j * rows2, rows2), :].astype(BF)
            c = copy(q, 1, k, s2.at[q, k - 1], r2.at[q, k - 1], at_plane(j))
            c.start()
            copies.append(c)
        return copies

    def stage2(q):
        total = acc1[q, rows_at(my_plane * rows2, rows2), :]
        for k in range(1, plane):
            total = total + r2[q, k - 1].astype(F32)
        acc2[q] = total
        copies = []
        if not scatter:
            r3[q, high] = total.astype(BF)
        for k in range(1, tall):
            j = lax.rem(high + k, tall)
            if scatter:
                s3[q, k - 1] = acc2[q, rows_at(j * rows3, rows3), :].astype(BF)
                c = copy(q, 2, k, s3.at[q, k - 1], r3.at[q, k - 1], at_tall(j))
            else:
                c = copy(q, 2, k, r3.at[q, high], r3.at[q, high], at_tall(j))
            c.start()
            copies.append(c)
        return copies

    def stage3(q):
        if scatter:
            total = acc2[q, rows_at(high * rows3, rows3), :]
            for k in range(1, tall):
                total = total + r3[q, k - 1].astype(F32)
        else:
            total = r3[q, 0].astype(F32)
            for j in range(1, tall):
                total = total + r3[q, j].astype(F32)
        gathered[q, rows_at(base3, rows3), :] = total.astype(BF)
        copies = []
        if scatter:
            chunk = gathered.at[q, rows_at(base3, rows3), :]
            for k in range(1, tall):
                c = copy(q, 3, k, chunk, chunk, at_tall(lax.rem(high + k, tall)))
                c.start()
                copies.append(c)
        return copies

    def stage4(q):
        chunk = gathered.at[q, rows_at(base2, rows2), :]
        copies = []
        for k in range(1, plane):
            c = copy(q, 4, k, chunk, chunk, at_plane(lax.rem(my_plane + k, plane)))
            c.start()
            copies.append(c)
        return copies

    def stage5(q):
        chunk = gathered.at[q, rows_at(base1, half), :]
        c = copy(q, 5, 1, chunk, chunk, at_core(1 - core))
        c.start()
        return [c]

    def finish(copies):
        for c in copies:
            c.wait()

    stages = [stage0, stage1, stage2, stage3, stage4, stage5]
    flying = [stage0(q) for q in range(pieces)]
    for number in range(1, len(stages)):
        for q in range(pieces):
            finish(flying[q])
            flying[q] = stages[number](q)
            if number == 1 and q == 0:
                eg[...] = (contract_cols(dz[...], w_neigh[...]) / degree).astype(BF)
                accum[...] = dot(count[verts:, :], eg[...])

                def fill(d, carry):
                    for h in range(hubs_own):
                        hub_send[d, pl.ds(h, 1), :] = accum[pl.ds(d * hubs_own + h, 1), :]
                    return carry

                lax.fori_loop(0, devices, fill, 0)
                for p in range(ns):
                    bound_send[p] = accum[pl.ds(hub_count + p * cap, cap), :]
                start_all(bound_copy(bound_send, bound_back, 3), ns)
                start_all(hub_return, devices)
            if number == 2 and q == 0:
                grad_features[...] = contract_cols(dz[...], w_self[...]) + dot(
                    count[:verts, :], eg[...]
                )
            if number == 4 and q == pieces - 1:
                back[...] = jnp.zeros_like(back)
                for i in range(cap):
                    back[pl.ds(shard * cap + i, 1), :] = bound_send[shard, pl.ds(i, 1), :]
                wait_all(bound_back, 3)
                for k in range(1, ns):
                    source = lax.rem(shard - k + ns, ns)
                    for i in range(cap):
                        back[pl.ds(source * cap + i, 1), :] = bound_back[k - 1, pl.ds(i, 1), :]
                wait_all(hub_back, 1)
                back[pl.ds(ns * cap, hubs_own), :] = hub_send[me] + jnp.sum(hub_back[...], axis=0)
                grad_features[...] = grad_features[...] + contract_rows(
                    pick[...].astype(BF), back[...].astype(BF)
                )
                stores.append(
                    pltpu.make_async_copy(grad_features, grad_features_hbm, store_sems.at[1])
                )
                stores[-1].start()
    for q in range(pieces):
        finish(flying[q])
        stores.append(
            pltpu.make_async_copy(gathered.at[q], gathered_hbm.at[q], store_sems.at[2 + q])
        )
        stores[-1].start()
    for store in stores:
        store.wait()


def writer(
    hidden_in, grad_features_in, gathered_in, hidden, grad_features, grad_self, grad_neigh,
    narrow, wide, hidden_held, grad_held, in_sems, out_sems,
):
    pieces, width, part = narrow.shape
    cuts = in_sems.shape[1]
    step = width // cuts
    places = [(q, i) for q in range(pieces) for i in range(cuts)]
    passed = (
        (hidden_in, hidden_held, hidden),
        (grad_features_in, grad_held, grad_features),
    )
    writes = []
    for i, (a, b, c) in enumerate(passed):
        pltpu.make_async_copy(a, b, in_sems.at[pieces, i]).start()
    reads = []
    for q, i in places:
        rows = pl.ds(i * step, step)
        reads.append(
            pltpu.make_async_copy(gathered_in.at[q, rows], narrow.at[q, rows], in_sems.at[q, i])
        )
        reads[-1].start()
    for i, (a, b, c) in enumerate(passed):
        pltpu.make_async_copy(a, b, in_sems.at[pieces, i]).wait()
        writes.append(pltpu.make_async_copy(b, c, out_sems.at[pieces, i]))
        writes[-1].start()
    for read, (q, i) in zip(reads, places):
        read.wait()
        rows = pl.ds(i * step, step)
        cols = pl.ds((q % COLUMN_PARTS) * part, part)
        wide[q, rows, :] = narrow[q, rows, :].astype(F32)
        out = grad_self if q // COLUMN_PARTS == 0 else grad_neigh
        writes.append(
            pltpu.make_async_copy(wide.at[q, rows], out.at[rows, cols], out_sems.at[q, i])
        )
        writes[-1].start()
    for c in writes:
        c.wait()


def body(nd, ns, features, w_self, w_neigh, cotangent, neighbours, hub_slots, send_rows, send_counts):
    verts, width = features.shape
    cap = send_rows.shape[2]
    hubs_own = hub_slots.shape[0]
    devices = nd * ns
    extra = round_up(hubs_own * devices + ns * cap, 128)
    picks = round_up(ns * cap + hubs_own, 16)
    pieces = 2 * COLUMN_PARTS
    part = width // COLUMN_PARTS
    plane = (nd // 2) * 2
    tall = ns // 2
    half = width // 2
    rows2 = half // plane
    scatter = rows2 % (tall * ROW_TILE) == 0
    rows3 = rows2 // tall if scatter else rows2
    landings = tall - 1 if scatter else tall
    most = max(plane, tall) - 1
    smem = pl.BlockSpec(memory_space=pltpu.SMEM)
    hbm = pl.BlockSpec(memory_space=pltpu.HBM)
    shapes = (
        jax.ShapeDtypeStruct((verts, width), BF),
        jax.ShapeDtypeStruct((verts, width), F32),
        jax.ShapeDtypeStruct((width, width), F32),
        jax.ShapeDtypeStruct((width, width), F32),
    )
    results = pl.pallas_call(
        functools.partial(kernel, nd, ns),
        out_shape=shapes[:2] + (jax.ShapeDtypeStruct((pieces, width, part), BF),),
        in_specs=[hbm] * 7 + [smem],
        out_specs=[hbm] * 3,
        scratch_shapes=[
            pltpu.VMEM((verts, width), BF),
            pltpu.VMEM((verts, width), F32),
            pltpu.SemaphoreType.DMA((2 + pieces,)),
            pltpu.VMEM((verts, width), BF),
            pltpu.VMEM((width, width), BF),
            pltpu.VMEM((width, width), BF),
            pltpu.VMEM((verts, width), BF),
            pltpu.VMEM((neighbours.shape[1], verts), jnp.int32),
            pltpu.SMEM((1, cap, ns), jnp.int32),
            pltpu.SMEM((1, ns), jnp.int32),
            pltpu.SemaphoreType.DMA((7,)),
            pltpu.VMEM((picks, verts), F32),
            pltpu.VMEM((picks, width), F32),
            pltpu.VMEM((hubs_own, width), F32),
            pltpu.VMEM((devices - 1, hubs_own, width), F32),
            pltpu.VMEM((ns, cap, width), F32),
            pltpu.VMEM((ns - 1, cap, width), F32),
            pltpu.VMEM((extra, width), F32),
            pltpu.VMEM((verts + extra, verts), BF),
            pltpu.VMEM((verts, width), BF),
            pltpu.VMEM((verts, width), F32),
            pltpu.VMEM((verts, width), BF),
            pltpu.VMEM((verts, width), BF),
            pltpu.VMEM((extra, width), F32),
            pltpu.VMEM((devices, hubs_own, width), F32),
            pltpu.VMEM((devices - 1, hubs_own, width), F32),
            pltpu.VMEM((ns, cap, width), F32),
            pltpu.VMEM((ns - 1, cap, width), F32),
            pltpu.VMEM((picks, width), F32),
            pltpu.VMEM((pieces, half, part), BF),
            pltpu.VMEM((pieces, half, part), BF),
            pltpu.VMEM((pieces, half, part), F32),
            pltpu.VMEM((pieces, plane - 1, rows2, part), BF),
            pltpu.VMEM((pieces, plane - 1, rows2, part), BF),
            pltpu.VMEM((pieces, rows2, part), F32),
            pltpu.VMEM((pieces, tall - 1, rows3, part), BF),
            pltpu.VMEM((pieces, landings, rows3, part), BF),
            pltpu.VMEM((pieces, width, part), BF),
            pltpu.SemaphoreType.DMA((4,)),
            pltpu.SemaphoreType.DMA((4,)),
            pltpu.SemaphoreType.DMA((pieces, 6, most)),
            pltpu.SemaphoreType.DMA((pieces, 6, most)),
        ],
        compiler_params=pltpu.CompilerParams(
            collective_id=0, has_side_effects=True, vmem_limit_bytes=VMEM_GRANT
        ),
    )(
        features, w_self, w_neigh, cotangent, neighbours.T, send_rows.transpose(0, 2, 1),
        send_counts, hub_slots,
    )
    return pl.pallas_call(
        writer,
        out_shape=shapes,
        in_specs=[hbm] * 3,
        out_specs=[hbm] * 4,
        scratch_shapes=[
            pltpu.VMEM((pieces, width, part), BF),
            pltpu.VMEM((pieces, width, part), F32),
            pltpu.VMEM((verts, width), BF),
            pltpu.VMEM((verts, width), F32),
            pltpu.SemaphoreType.DMA((pieces + 1, 2)),
            pltpu.SemaphoreType.DMA((pieces + 1, 2)),
        ],
        compiler_params=pltpu.CompilerParams(vmem_limit_bytes=VMEM_GRANT),
    )(*results)


def solution(mesh):
    both = ("dom", "shard")
    return jax.shard_map(
        functools.partial(body, mesh.shape["dom"], mesh.shape["shard"]),
        mesh=mesh,
        in_specs=(
            P(both, None),
            P(),
            P(),
            P(both, None),
            P(both, None),
            P(both),
            P(both, None, None),
            P(both, None),
        ),
        out_specs=(P(both, None), P(both, None), P(), P()),
        check_vma=False,
    )
```

```python
import functools

import jax
import jax.numpy as jnp
from jax import lax
from jax.experimental import pallas as pl
from jax.experimental.pallas import tpu as pltpu
from jax.sharding import PartitionSpec as P

BF = jnp.bfloat16
F32 = jnp.float32
MESH = pl.DeviceIdType.MESH
COLUMN_PARTS = 2
ROW_TILE = 16
VMEM_GRANT = 60 * 1024 * 1024


def contract_rows(left, right):
    return lax.dot_general(left, right, (((0,), (0,)), ((), ())), preferred_element_type=F32)


def contract_cols(left, right):
    return lax.dot_general(left, right, (((1,), (1,)), ((), ())), preferred_element_type=F32)


def dot(left, right):
    return jnp.dot(left, right, preferred_element_type=F32)


def round_up(value, step):
    return -(-value // step) * step


def kernel(
    nd, ns,
    features_hbm, w_self_hbm, w_neigh_hbm, cotangent_hbm, neighbours_hbm, rows_hbm, counts_hbm,
    hub_slots,
    hidden_hbm, grad_features_hbm, gathered_hbm,
    hidden, grad_features, store_sems,
    features, w_self, w_neigh, cotangent, neighbours, send_rows, send_counts, load_sems,
    pick, picked, hub_out, hub_in, bound_out, bound_in, table, count, agg, zs, dz, eg, accum,
    hub_send, hub_back, bound_send, bound_back, back,
    s1, r1, acc1, s2, r2, acc2, s3, r3, gathered,
    small_send, small_recv, send_sems, recv_sems,
):
    verts, width = features.shape
    slots = neighbours.shape[0]
    devices = nd * ns
    cap = send_rows.shape[1]
    hubs_own = hub_slots.shape[0]
    hub_count = hubs_own * devices
    live_rows = hub_count + ns * cap
    table_size = verts + live_rows
    dom = lax.axis_index("dom")
    shard = lax.axis_index("shard")
    me = dom * ns + shard
    core = lax.rem(dom, 2)
    y = lax.div(dom, 2)
    low = lax.rem(shard, 2)
    high = lax.div(shard, 2)

    def device_of(index):
        return (lax.div(index, ns), lax.rem(index, ns))

    pairs = (
        (rows_hbm, send_rows),
        (counts_hbm, send_counts),
        (features_hbm, features),
        (neighbours_hbm, neighbours),
        (w_self_hbm, w_self),
        (w_neigh_hbm, w_neigh),
        (cotangent_hbm, cotangent),
    )
    loads = [pltpu.make_async_copy(a, b, load_sems.at[i]) for i, (a, b) in enumerate(pairs)]
    for load in loads:
        load.start()

    barrier = pltpu.get_barrier_semaphore()

    def greet(k, carry):
        pl.semaphore_signal(
            barrier, inc=1, device_id=device_of(lax.rem(me + k, devices)), device_id_type=MESH
        )
        return carry

    lax.fori_loop(1, devices, greet, 0)

    lane = lax.broadcasted_iota(jnp.int32, (1, verts), 1)
    pick[...] = jnp.zeros_like(pick)
    loads[0].wait()
    loads[1].wait()
    for p in range(ns):
        for k in range(cap):
            row = jnp.where(k < send_counts[0, p], send_rows[0, k, p], -1)
            pick[pl.ds(p * cap + k, 1), :] = (lane == row).astype(F32)
    for h in range(hubs_own):
        pick[pl.ds(ns * cap + h, 1), :] = (lane == hub_slots[h]).astype(F32)
    loads[2].wait()
    picked[...] = dot(pick[...].astype(BF), features[...])
    for p in range(ns):
        bound_out[p] = picked[pl.ds(p * cap, cap), :]
    hub_out[...] = picked[pl.ds(ns * cap, hubs_own), :]

    pl.semaphore_wait(barrier, devices - 1)

    def hub_copy(k):
        return pltpu.make_async_remote_copy(
            src_ref=hub_out,
            dst_ref=hub_in.at[k - 1],
            send_sem=small_send.at[0],
            recv_sem=small_recv.at[0],
            device_id=device_of(lax.rem(me + k, devices)),
            device_id_type=MESH,
        )

    def hub_return(k):
        target = lax.rem(me + k, devices)
        return pltpu.make_async_remote_copy(
            src_ref=hub_send.at[target],
            dst_ref=hub_back.at[k - 1],
            send_sem=small_send.at[1],
            recv_sem=small_recv.at[1],
            device_id=device_of(target),
            device_id_type=MESH,
        )

    def bound_copy(source, landing, number):
        def make(k):
            target = lax.rem(shard + k, ns)
            return pltpu.make_async_remote_copy(
                src_ref=source.at[target],
                dst_ref=landing.at[k - 1],
                send_sem=small_send.at[number],
                recv_sem=small_recv.at[number],
                device_id=(dom, target),
                device_id_type=MESH,
            )

        return make

    def start_all(make, total):
        def one(k, carry):
            make(k).start()
            return carry

        lax.fori_loop(1, total, one, 0)

    def wait_all(landing, number):
        pltpu.make_async_copy(landing, landing, small_recv.at[number]).wait()
        pltpu.make_async_copy(landing, landing, small_send.at[number]).wait()

    start_all(bound_copy(bound_out, bound_in, 2), ns)
    start_all(hub_copy, devices)

    block = 64
    names = lax.broadcasted_iota(jnp.int32, (block, verts), 0)
    loads[3].wait()

    def count_block(i, carry):
        first = pl.multiple_of(i * block, block)
        total = jnp.zeros((block, verts), F32)
        for j in range(slots):
            total = total + (neighbours[pl.ds(j, 1), :] - first == names).astype(F32)
        count[pl.ds(first, block), :] = total.astype(BF)
        return carry

    lax.fori_loop(0, count.shape[0] // block, count_block, 0)
    alive = (neighbours[...] < table_size).astype(F32).astype(BF)
    degree = contract_rows(alive, jnp.ones((slots, 128), BF))
    degree = jnp.concatenate([degree] * (width // 128), axis=1)
    loads[4].wait()
    zs[...] = dot(features[...], w_self[...])
    local_sums = contract_rows(count[:verts, :], features[...])

    table[...] = jnp.zeros_like(table)
    for h in range(hubs_own):
        table[pl.ds(me * hubs_own + h, 1), :] = hub_out[pl.ds(h, 1), :]
    for k in range(cap):
        table[pl.ds(hub_count + shard * cap + k, 1), :] = bound_out[shard, pl.ds(k, 1), :]
    wait_all(bound_in, 2)
    for k in range(1, ns):
        source = lax.rem(shard - k + ns, ns)
        for i in range(cap):
            table[pl.ds(hub_count + source * cap + i, 1), :] = bound_in[k - 1, pl.ds(i, 1), :]
    wait_all(hub_in, 0)

    def place_hub(k, carry):
        source = lax.rem(me - k + devices, devices)
        for h in range(hubs_own):
            table[pl.ds(source * hubs_own + h, 1), :] = hub_in[k - 1, pl.ds(h, 1), :]
        return carry

    lax.fori_loop(1, devices, place_hub, 0)

    loads[5].wait()
    loads[6].wait()
    sums = local_sums + contract_rows(count[verts:, :], table[...].astype(BF))
    agg[...] = (sums / degree).astype(BF)
    z = zs[...] + dot(agg[...], w_neigh[...])
    sig = jax.nn.sigmoid(z)
    hidden[...] = (z * sig).astype(BF)
    stores = [pltpu.make_async_copy(hidden, hidden_hbm, store_sems.at[0])]
    stores[0].start()
    dz[...] = (cotangent[...].astype(F32) * sig * (1.0 + z * (1.0 - sig))).astype(BF)

    part = width // COLUMN_PARTS
    pieces = 2 * COLUMN_PARTS
    plane = (nd // 2) * 2
    tall = ns // 2
    half = width // 2
    rows2 = half // plane
    scatter = rows2 % (tall * ROW_TILE) == 0
    rows3 = rows2 // tall if scatter else rows2
    my_plane = y * 2 + low
    base1 = core * half
    base2 = base1 + my_plane * rows2
    base3 = base2 + high * rows3 if scatter else base2

    def at_core(j):
        return (y * 2 + j, shard)

    def at_plane(j):
        return (lax.div(j, 2) * 2 + core, high * 2 + lax.rem(j, 2))

    def at_tall(j):
        return (dom, j * 2 + low)

    def copy(q, stage, k, source, landing, target):
        return pltpu.make_async_remote_copy(
            src_ref=source,
            dst_ref=landing,
            send_sem=send_sems.at[q, stage, k - 1],
            recv_sem=recv_sems.at[q, stage, k - 1],
            device_id=target,
            device_id_type=MESH,
        )

    def rows_at(start, size):
        return pl.ds(pl.multiple_of(start, ROW_TILE), size)

    def left_of(q):
        return features if q // COLUMN_PARTS == 0 else agg

    def right_of(q):
        return dz[:, pl.ds((q % COLUMN_PARTS) * part, part)]

    def stage0(q):
        other = pl.ds(pl.multiple_of((1 - core) * half, half), half)
        own = pl.ds(pl.multiple_of(core * half, half), half)
        s1[q] = contract_rows(left_of(q)[:, other], right_of(q)).astype(BF)
        c = copy(q, 0, 1, s1.at[q], r1.at[q], at_core(1 - core))
        c.start()
        acc1[q] = contract_rows(left_of(q)[:, own], right_of(q))
        return [c]

    def stage1(q):
        acc1[q] = acc1[q] + r1[q].astype(F32)
        copies = []
        for k in range(1, plane):
            j = lax.rem(my_plane + k, plane)
            s2[q, k - 1] = acc1[q, rows_at(j * rows2, rows2), :].astype(BF)
            c = copy(q, 1, k, s2.at[q, k - 1], r2.at[q, k - 1], at_plane(j))
            c.start()
            copies.append(c)
        return copies

    def stage2(q):
        total = acc1[q, rows_at(my_plane * rows2, rows2), :]
        for k in range(1, plane):
            total = total + r2[q, k - 1].astype(F32)
        acc2[q] = total
        copies = []
        if not scatter:
            r3[q, high] = total.astype(BF)
        for k in range(1, tall):
            j = lax.rem(high + k, tall)
            if scatter:
                s3[q, k - 1] = acc2[q, rows_at(j * rows3, rows3), :].astype(BF)
                c = copy(q, 2, k, s3.at[q, k - 1], r3.at[q, k - 1], at_tall(j))
            else:
                c = copy(q, 2, k, r3.at[q, high], r3.at[q, high], at_tall(j))
            c.start()
            copies.append(c)
        return copies

    def stage3(q):
        if scatter:
            total = acc2[q, rows_at(high * rows3, rows3), :]
            for k in range(1, tall):
                total = total + r3[q, k - 1].astype(F32)
        else:
            total = r3[q, 0].astype(F32)
            for j in range(1, tall):
                total = total + r3[q, j].astype(F32)
        gathered[q, rows_at(base3, rows3), :] = total.astype(BF)
        copies = []
        if scatter:
            chunk = gathered.at[q, rows_at(base3, rows3), :]
            for k in range(1, tall):
                c = copy(q, 3, k, chunk, chunk, at_tall(lax.rem(high + k, tall)))
                c.start()
                copies.append(c)
        return copies

    def stage4(q):
        chunk = gathered.at[q, rows_at(base2, rows2), :]
        copies = []
        for k in range(1, plane):
            c = copy(q, 4, k, chunk, chunk, at_plane(lax.rem(my_plane + k, plane)))
            c.start()
            copies.append(c)
        return copies

    def stage5(q):
        chunk = gathered.at[q, rows_at(base1, half), :]
        c = copy(q, 5, 1, chunk, chunk, at_core(1 - core))
        c.start()
        return [c]

    def finish(copies):
        for c in copies:
            c.wait()

    stages = [stage0, stage1, stage2, stage3, stage4, stage5]
    flying = [stage0(0)]
    for number in range(1, len(stages)):
        for q in range(pieces):
            if number == 1 and q + 1 < pieces:
                flying.append(stage0(q + 1))
            finish(flying[q])
            flying[q] = stages[number](q)
            if number == 1 and q == pieces - 1:
                eg[...] = (contract_cols(dz[...], w_neigh[...]) / degree).astype(BF)
                accum[...] = dot(count[verts:, :], eg[...])

                def fill(d, carry):
                    for h in range(hubs_own):
                        hub_send[d, pl.ds(h, 1), :] = accum[pl.ds(d * hubs_own + h, 1), :]
                    return carry

                lax.fori_loop(0, devices, fill, 0)
                for p in range(ns):
                    bound_send[p] = accum[pl.ds(hub_count + p * cap, cap), :]
                start_all(bound_copy(bound_send, bound_back, 3), ns)
                start_all(hub_return, devices)
                grad_features[...] = contract_cols(dz[...], w_self[...]) + dot(
                    count[:verts, :], eg[...]
                )
            if number == 4 and q == pieces - 1:
                back[...] = jnp.zeros_like(back)
                for i in range(cap):
                    back[pl.ds(shard * cap + i, 1), :] = bound_send[shard, pl.ds(i, 1), :]
                wait_all(bound_back, 3)
                for k in range(1, ns):
                    source = lax.rem(shard - k + ns, ns)
                    for i in range(cap):
                        back[pl.ds(source * cap + i, 1), :] = bound_back[k - 1, pl.ds(i, 1), :]
                wait_all(hub_back, 1)
                back[pl.ds(ns * cap, hubs_own), :] = hub_send[me] + jnp.sum(hub_back[...], axis=0)
                grad_features[...] = grad_features[...] + contract_rows(
                    pick[...].astype(BF), back[...].astype(BF)
                )
                stores.append(
                    pltpu.make_async_copy(grad_features, grad_features_hbm, store_sems.at[1])
                )
                stores[-1].start()
    for q in range(pieces):
        finish(flying[q])
        stores.append(
            pltpu.make_async_copy(gathered.at[q], gathered_hbm.at[q], store_sems.at[2 + q])
        )
        stores[-1].start()
    for store in stores:
        store.wait()


def writer(
    hidden_in, grad_features_in, gathered_in, hidden, grad_features, grad_self, grad_neigh,
    narrow, wide, hidden_held, grad_held, in_sems, out_sems,
):
    pieces, width, part = narrow.shape
    cuts = in_sems.shape[1]
    step = width // cuts
    places = [(q, i) for q in range(pieces) for i in range(cuts)]
    passed = (
        (hidden_in, hidden_held, hidden),
        (grad_features_in, grad_held, grad_features),
    )
    writes = []
    for i, (a, b, c) in enumerate(passed):
        pltpu.make_async_copy(a, b, in_sems.at[pieces, i]).start()
    reads = []
    for q, i in places:
        rows = pl.ds(i * step, step)
        reads.append(
            pltpu.make_async_copy(gathered_in.at[q, rows], narrow.at[q, rows], in_sems.at[q, i])
        )
        reads[-1].start()
    for i, (a, b, c) in enumerate(passed):
        pltpu.make_async_copy(a, b, in_sems.at[pieces, i]).wait()
        writes.append(pltpu.make_async_copy(b, c, out_sems.at[pieces, i]))
        writes[-1].start()
    for read, (q, i) in zip(reads, places):
        read.wait()
        rows = pl.ds(i * step, step)
        cols = pl.ds((q % COLUMN_PARTS) * part, part)
        wide[q, rows, :] = narrow[q, rows, :].astype(F32)
        out = grad_self if q // COLUMN_PARTS == 0 else grad_neigh
        writes.append(
            pltpu.make_async_copy(wide.at[q, rows], out.at[rows, cols], out_sems.at[q, i])
        )
        writes[-1].start()
    for c in writes:
        c.wait()


def body(nd, ns, features, w_self, w_neigh, cotangent, neighbours, hub_slots, send_rows, send_counts):
    verts, width = features.shape
    cap = send_rows.shape[2]
    hubs_own = hub_slots.shape[0]
    devices = nd * ns
    extra = round_up(hubs_own * devices + ns * cap, 128)
    picks = round_up(ns * cap + hubs_own, 16)
    pieces = 2 * COLUMN_PARTS
    part = width // COLUMN_PARTS
    plane = (nd // 2) * 2
    tall = ns // 2
    half = width // 2
    rows2 = half // plane
    scatter = rows2 % (tall * ROW_TILE) == 0
    rows3 = rows2 // tall if scatter else rows2
    landings = tall - 1 if scatter else tall
    most = max(plane, tall) - 1
    smem = pl.BlockSpec(memory_space=pltpu.SMEM)
    hbm = pl.BlockSpec(memory_space=pltpu.HBM)
    shapes = (
        jax.ShapeDtypeStruct((verts, width), BF),
        jax.ShapeDtypeStruct((verts, width), F32),
        jax.ShapeDtypeStruct((width, width), F32),
        jax.ShapeDtypeStruct((width, width), F32),
    )
    results = pl.pallas_call(
        functools.partial(kernel, nd, ns),
        out_shape=shapes[:2] + (jax.ShapeDtypeStruct((pieces, width, part), BF),),
        in_specs=[hbm] * 7 + [smem],
        out_specs=[hbm] * 3,
        scratch_shapes=[
            pltpu.VMEM((verts, width), BF),
            pltpu.VMEM((verts, width), F32),
            pltpu.SemaphoreType.DMA((2 + pieces,)),
            pltpu.VMEM((verts, width), BF),
            pltpu.VMEM((width, width), BF),
            pltpu.VMEM((width, width), BF),
            pltpu.VMEM((verts, width), BF),
            pltpu.VMEM((neighbours.shape[1], verts), jnp.int32),
            pltpu.SMEM((1, cap, ns), jnp.int32),
            pltpu.SMEM((1, ns), jnp.int32),
            pltpu.SemaphoreType.DMA((7,)),
            pltpu.VMEM((picks, verts), F32),
            pltpu.VMEM((picks, width), F32),
            pltpu.VMEM((hubs_own, width), F32),
            pltpu.VMEM((devices - 1, hubs_own, width), F32),
            pltpu.VMEM((ns, cap, width), F32),
            pltpu.VMEM((ns - 1, cap, width), F32),
            pltpu.VMEM((extra, width), F32),
            pltpu.VMEM((verts + extra, verts), BF),
            pltpu.VMEM((verts, width), BF),
            pltpu.VMEM((verts, width), F32),
            pltpu.VMEM((verts, width), BF),
            pltpu.VMEM((verts, width), BF),
            pltpu.VMEM((extra, width), F32),
            pltpu.VMEM((devices, hubs_own, width), F32),
            pltpu.VMEM((devices - 1, hubs_own, width), F32),
            pltpu.VMEM((ns, cap, width), F32),
            pltpu.VMEM((ns - 1, cap, width), F32),
            pltpu.VMEM((picks, width), F32),
            pltpu.VMEM((pieces, half, part), BF),
            pltpu.VMEM((pieces, half, part), BF),
            pltpu.VMEM((pieces, half, part), F32),
            pltpu.VMEM((pieces, plane - 1, rows2, part), BF),
            pltpu.VMEM((pieces, plane - 1, rows2, part), BF),
            pltpu.VMEM((pieces, rows2, part), F32),
            pltpu.VMEM((pieces, tall - 1, rows3, part), BF),
            pltpu.VMEM((pieces, landings, rows3, part), BF),
            pltpu.VMEM((pieces, width, part), BF),
            pltpu.SemaphoreType.DMA((4,)),
            pltpu.SemaphoreType.DMA((4,)),
            pltpu.SemaphoreType.DMA((pieces, 6, most)),
            pltpu.SemaphoreType.DMA((pieces, 6, most)),
        ],
        compiler_params=pltpu.CompilerParams(
            collective_id=0, has_side_effects=True, vmem_limit_bytes=VMEM_GRANT
        ),
    )(
        features, w_self, w_neigh, cotangent, neighbours.T, send_rows.transpose(0, 2, 1),
        send_counts, hub_slots,
    )
    return pl.pallas_call(
        writer,
        out_shape=shapes,
        in_specs=[hbm] * 3,
        out_specs=[hbm] * 4,
        scratch_shapes=[
            pltpu.VMEM((pieces, width, part), BF),
            pltpu.VMEM((pieces, width, part), F32),
            pltpu.VMEM((verts, width), BF),
            pltpu.VMEM((verts, width), F32),
            pltpu.SemaphoreType.DMA((pieces + 1, 2)),
            pltpu.SemaphoreType.DMA((pieces + 1, 2)),
        ],
        compiler_params=pltpu.CompilerParams(vmem_limit_bytes=VMEM_GRANT),
    )(*results)


def solution(mesh):
    both = ("dom", "shard")
    return jax.shard_map(
        functools.partial(body, mesh.shape["dom"], mesh.shape["shard"]),
        mesh=mesh,
        in_specs=(
            P(both, None),
            P(),
            P(),
            P(both, None),
            P(both, None),
            P(both),
            P(both, None, None),
            P(both, None),
        ),
        out_specs=(P(both, None), P(both, None), P(), P()),
        check_vma=False,
    )
```

```python
import functools

import jax
import jax.numpy as jnp
from jax import lax
from jax.experimental import pallas as pl
from jax.experimental.pallas import tpu as pltpu
from jax.sharding import PartitionSpec as P

BF = jnp.bfloat16
F32 = jnp.float32
MESH = pl.DeviceIdType.MESH
COLUMN_PARTS = 2
ROW_TILE = 16
VMEM_GRANT = 60 * 1024 * 1024


def contract_rows(left, right):
    return lax.dot_general(left, right, (((0,), (0,)), ((), ())), preferred_element_type=F32)


def contract_cols(left, right):
    return lax.dot_general(left, right, (((1,), (1,)), ((), ())), preferred_element_type=F32)


def dot(left, right):
    return jnp.dot(left, right, preferred_element_type=F32)


def round_up(value, step):
    return -(-value // step) * step


def kernel(
    nd, ns,
    features_hbm, w_self_hbm, w_neigh_hbm, cotangent_hbm, neighbours_hbm, rows_hbm, counts_hbm,
    hub_slots,
    hidden_hbm, grad_features_hbm, gathered_hbm,
    hidden, grad_features, features_t, store_sems,
    features, w_self, w_neigh, cotangent, neighbours, send_rows, send_counts, load_sems,
    pick, picked, hub_out, hub_in, bound_out, bound_in, table, count, agg, zs, dz, eg, accum,
    hub_send, hub_back, bound_send, bound_back, back,
    s1, r1, acc1, s2, r2, acc2, s3, r3, gathered,
    small_send, small_recv, send_sems, recv_sems,
):
    verts, width = features.shape
    slots = neighbours.shape[0]
    devices = nd * ns
    cap = send_rows.shape[1]
    hubs_own = hub_slots.shape[0]
    hub_count = hubs_own * devices
    live_rows = hub_count + ns * cap
    table_size = verts + live_rows
    dom = lax.axis_index("dom")
    shard = lax.axis_index("shard")
    me = dom * ns + shard
    core = lax.rem(dom, 2)
    y = lax.div(dom, 2)
    low = lax.rem(shard, 2)
    high = lax.div(shard, 2)

    def device_of(index):
        return (lax.div(index, ns), lax.rem(index, ns))

    pairs = (
        (rows_hbm, send_rows),
        (counts_hbm, send_counts),
        (features_hbm, features),
        (neighbours_hbm, neighbours),
        (w_self_hbm, w_self),
        (w_neigh_hbm, w_neigh),
        (cotangent_hbm, cotangent),
    )
    loads = [pltpu.make_async_copy(a, b, load_sems.at[i]) for i, (a, b) in enumerate(pairs)]
    for load in loads:
        load.start()

    barrier = pltpu.get_barrier_semaphore()

    def greet(k, carry):
        pl.semaphore_signal(
            barrier, inc=1, device_id=device_of(lax.rem(me + k, devices)), device_id_type=MESH
        )
        return carry

    lax.fori_loop(1, devices, greet, 0)

    lane = lax.broadcasted_iota(jnp.int32, (1, verts), 1)
    pick[...] = jnp.zeros_like(pick)
    loads[0].wait()
    loads[1].wait()
    for p in range(ns):
        for k in range(cap):
            row = jnp.where(k < send_counts[0, p], send_rows[0, k, p], -1)
            pick[pl.ds(p * cap + k, 1), :] = (lane == row).astype(F32)
    for h in range(hubs_own):
        pick[pl.ds(ns * cap + h, 1), :] = (lane == hub_slots[h]).astype(F32)
    loads[2].wait()
    picked[...] = dot(pick[...].astype(BF), features[...])
    for p in range(ns):
        bound_out[p] = picked[pl.ds(p * cap, cap), :]
    hub_out[...] = picked[pl.ds(ns * cap, hubs_own), :]

    pl.semaphore_wait(barrier, devices - 1)

    def hub_copy(k):
        return pltpu.make_async_remote_copy(
            src_ref=hub_out,
            dst_ref=hub_in.at[k - 1],
            send_sem=small_send.at[0],
            recv_sem=small_recv.at[0],
            device_id=device_of(lax.rem(me + k, devices)),
            device_id_type=MESH,
        )

    def hub_return(k):
        target = lax.rem(me + k, devices)
        return pltpu.make_async_remote_copy(
            src_ref=hub_send.at[target],
            dst_ref=hub_back.at[k - 1],
            send_sem=small_send.at[1],
            recv_sem=small_recv.at[1],
            device_id=device_of(target),
            device_id_type=MESH,
        )

    def bound_copy(source, landing, number):
        def make(k):
            target = lax.rem(shard + k, ns)
            return pltpu.make_async_remote_copy(
                src_ref=source.at[target],
                dst_ref=landing.at[k - 1],
                send_sem=small_send.at[number],
                recv_sem=small_recv.at[number],
                device_id=(dom, target),
                device_id_type=MESH,
            )

        return make

    def start_all(make, total):
        def one(k, carry):
            make(k).start()
            return carry

        lax.fori_loop(1, total, one, 0)

    def wait_all(landing, number):
        pltpu.make_async_copy(landing, landing, small_recv.at[number]).wait()
        pltpu.make_async_copy(landing, landing, small_send.at[number]).wait()

    start_all(bound_copy(bound_out, bound_in, 2), ns)
    start_all(hub_copy, devices)

    block = 64
    names = lax.broadcasted_iota(jnp.int32, (block, verts), 0)
    loads[3].wait()

    def count_block(i, carry):
        first = pl.multiple_of(i * block, block)
        total = jnp.zeros((block, verts), F32)
        for j in range(slots):
            total = total + (neighbours[pl.ds(j, 1), :] - first == names).astype(F32)
        count[pl.ds(first, block), :] = total.astype(BF)
        return carry

    lax.fori_loop(0, count.shape[0] // block, count_block, 0)
    alive = (neighbours[...] < table_size).astype(F32).astype(BF)
    degree = contract_rows(alive, jnp.ones((slots, 128), BF))
    inverse = jnp.concatenate([1.0 / degree] * (width // 128), axis=1)
    features_t[...] = features[...].T
    loads[4].wait()
    zs[...] = dot(features[...], w_self[...])
    local_sums = contract_rows(count[:verts, :], features[...])

    table[...] = jnp.zeros_like(table)
    for h in range(hubs_own):
        table[pl.ds(me * hubs_own + h, 1), :] = hub_out[pl.ds(h, 1), :]
    for k in range(cap):
        table[pl.ds(hub_count + shard * cap + k, 1), :] = bound_out[shard, pl.ds(k, 1), :]
    wait_all(bound_in, 2)
    for k in range(1, ns):
        source = lax.rem(shard - k + ns, ns)
        for i in range(cap):
            table[pl.ds(hub_count + source * cap + i, 1), :] = bound_in[k - 1, pl.ds(i, 1), :]
    wait_all(hub_in, 0)

    def place_hub(k, carry):
        source = lax.rem(me - k + devices, devices)
        for h in range(hubs_own):
            table[pl.ds(source * hubs_own + h, 1), :] = hub_in[k - 1, pl.ds(h, 1), :]
        return carry

    lax.fori_loop(1, devices, place_hub, 0)

    loads[5].wait()
    loads[6].wait()
    sums = local_sums + contract_rows(count[verts:, :], table[...].astype(BF))
    agg[...] = (sums * inverse).astype(BF)
    z = zs[...] + dot(agg[...], w_neigh[...])
    sig = jax.nn.sigmoid(z)
    hidden[...] = (z * sig).astype(BF)
    stores = [pltpu.make_async_copy(hidden, hidden_hbm, store_sems.at[0])]
    stores[0].start()
    dz[...] = (cotangent[...].astype(F32) * sig * (1.0 + z * (1.0 - sig))).astype(BF)

    part = width // COLUMN_PARTS
    pieces = 2 * COLUMN_PARTS
    plane = (nd // 2) * 2
    tall = ns // 2
    half = width // 2
    rows2 = half // plane
    scatter = rows2 % (tall * ROW_TILE) == 0
    rows3 = rows2 // tall if scatter else rows2
    my_plane = y * 2 + low
    base1 = core * half

    def at_core(j):
        return (y * 2 + j, shard)

    def at_plane(j):
        return (lax.div(j, 2) * 2 + core, high * 2 + lax.rem(j, 2))

    def at_tall(j):
        return (dom, j * 2 + low)

    def route(q):
        first, second = (plane, my_plane, at_plane), (tall, high, at_tall)
        if plane == tall and q == pieces // 2 and pieces > 2:
            return second, first
        return first, second

    def base2(q):
        return base1 + route(q)[0][1] * rows2

    def base3(q):
        return base2(q) + route(q)[1][1] * rows3 if scatter else base2(q)

    def copy(q, stage, k, source, landing, target):
        return pltpu.make_async_remote_copy(
            src_ref=source,
            dst_ref=landing,
            send_sem=send_sems.at[q, stage, k - 1],
            recv_sem=recv_sems.at[q, stage, k - 1],
            device_id=target,
            device_id_type=MESH,
        )

    def rows_at(start, size):
        return pl.ds(pl.multiple_of(start, ROW_TILE), size)

    def right_of(q):
        return dz[:, pl.ds((q % COLUMN_PARTS) * part, part)]

    def stage0(q):
        other = pl.ds(pl.multiple_of((1 - core) * half, half), half)
        own = pl.ds(pl.multiple_of(core * half, half), half)
        turned = q // COLUMN_PARTS == 0

        def product(rows):
            if turned:
                return dot(features_t[rows, :], right_of(q))
            return contract_rows(agg[:, rows], right_of(q))

        s1[q] = product(other).astype(BF)
        c = copy(q, 0, 1, s1.at[q], r1.at[q], at_core(1 - core))
        c.start()
        acc1[q] = product(own)
        return [c]

    def stage1(q):
        size, mine, at = route(q)[0]
        acc1[q] = acc1[q] + r1[q].astype(F32)
        copies = []
        for k in range(1, size):
            j = lax.rem(mine + k, size)
            s2[q, k - 1] = acc1[q, rows_at(j * rows2, rows2), :].astype(BF)
            c = copy(q, 1, k, s2.at[q, k - 1], r2.at[q, k - 1], at(j))
            c.start()
            copies.append(c)
        return copies

    def stage2(q):
        before, mine, _ = route(q)[0]
        total = acc1[q, rows_at(mine * rows2, rows2), :]
        for k in range(1, before):
            total = total + r2[q, k - 1].astype(F32)
        acc2[q] = total
        size, mine, at = route(q)[1]
        copies = []
        if not scatter:
            r3[q, mine] = total.astype(BF)
        for k in range(1, size):
            j = lax.rem(mine + k, size)
            if scatter:
                s3[q, k - 1] = acc2[q, rows_at(j * rows3, rows3), :].astype(BF)
                c = copy(q, 2, k, s3.at[q, k - 1], r3.at[q, k - 1], at(j))
            else:
                c = copy(q, 2, k, r3.at[q, mine], r3.at[q, mine], at(j))
            c.start()
            copies.append(c)
        return copies

    def stage3(q):
        size, mine, at = route(q)[1]
        if scatter:
            total = acc2[q, rows_at(mine * rows3, rows3), :]
            for k in range(1, size):
                total = total + r3[q, k - 1].astype(F32)
        else:
            total = r3[q, 0].astype(F32)
            for j in range(1, size):
                total = total + r3[q, j].astype(F32)
        gathered[q, rows_at(base3(q), rows3), :] = total.astype(BF)
        copies = []
        if scatter:
            chunk = gathered.at[q, rows_at(base3(q), rows3), :]
            for k in range(1, size):
                c = copy(q, 3, k, chunk, chunk, at(lax.rem(mine + k, size)))
                c.start()
                copies.append(c)
        return copies

    def stage4(q):
        size, mine, at = route(q)[0]
        chunk = gathered.at[q, rows_at(base2(q), rows2), :]
        copies = []
        for k in range(1, size):
            c = copy(q, 4, k, chunk, chunk, at(lax.rem(mine + k, size)))
            c.start()
            copies.append(c)
        return copies

    def stage5(q):
        chunk = gathered.at[q, rows_at(base1, half), :]
        c = copy(q, 5, 1, chunk, chunk, at_core(1 - core))
        c.start()
        return [c]

    def finish(copies):
        for c in copies:
            c.wait()

    stages = [stage0, stage1, stage2, stage3, stage4, stage5]
    flying = [stage0(0)]
    for number in range(1, len(stages)):
        for q in range(pieces):
            if number == 1 and q + 1 < pieces:
                flying.append(stage0(q + 1))
            finish(flying[q])
            flying[q] = stages[number](q)
            if number == 1 and q == pieces - 1:
                eg[...] = (contract_cols(dz[...], w_neigh[...]) * inverse).astype(BF)
                accum[...] = dot(count[verts:, :], eg[...])

                def fill(d, carry):
                    for h in range(hubs_own):
                        hub_send[d, pl.ds(h, 1), :] = accum[pl.ds(d * hubs_own + h, 1), :]
                    return carry

                lax.fori_loop(0, devices, fill, 0)
                for p in range(ns):
                    bound_send[p] = accum[pl.ds(hub_count + p * cap, cap), :]
                start_all(bound_copy(bound_send, bound_back, 3), ns)
                start_all(hub_return, devices)
                grad_features[...] = contract_cols(dz[...], w_self[...]) + dot(
                    count[:verts, :], eg[...]
                )
            if number == 4 and q == pieces - 1:
                back[...] = jnp.zeros_like(back)
                for i in range(cap):
                    back[pl.ds(shard * cap + i, 1), :] = bound_send[shard, pl.ds(i, 1), :]
                wait_all(bound_back, 3)
                for k in range(1, ns):
                    source = lax.rem(shard - k + ns, ns)
                    for i in range(cap):
                        back[pl.ds(source * cap + i, 1), :] = bound_back[k - 1, pl.ds(i, 1), :]
                wait_all(hub_back, 1)
                back[pl.ds(ns * cap, hubs_own), :] = hub_send[me] + jnp.sum(hub_back[...], axis=0)
                grad_features[...] = grad_features[...] + contract_rows(
                    pick[...].astype(BF), back[...].astype(BF)
                )
                stores.append(
                    pltpu.make_async_copy(grad_features, grad_features_hbm, store_sems.at[1])
                )
                stores[-1].start()
    for q in range(pieces):
        finish(flying[q])
        stores.append(
            pltpu.make_async_copy(gathered.at[q], gathered_hbm.at[q], store_sems.at[2 + q])
        )
        stores[-1].start()
    for store in stores:
        store.wait()


def writer(
    hidden_in, grad_features_in, gathered_in, hidden, grad_features, grad_self, grad_neigh,
    narrow, wide, hidden_held, grad_held, in_sems, out_sems,
):
    pieces, width, part = narrow.shape
    cuts = in_sems.shape[1]
    step = width // cuts
    places = [(q, i) for q in range(pieces) for i in range(cuts)]
    passed = (
        (hidden_in, hidden_held, hidden),
        (grad_features_in, grad_held, grad_features),
    )
    writes = []
    for i, (a, b, c) in enumerate(passed):
        pltpu.make_async_copy(a, b, in_sems.at[pieces, i]).start()
    reads = []
    for q, i in places:
        rows = pl.ds(i * step, step)
        reads.append(
            pltpu.make_async_copy(gathered_in.at[q, rows], narrow.at[q, rows], in_sems.at[q, i])
        )
        reads[-1].start()
    for i, (a, b, c) in enumerate(passed):
        pltpu.make_async_copy(a, b, in_sems.at[pieces, i]).wait()
        writes.append(pltpu.make_async_copy(b, c, out_sems.at[pieces, i]))
        writes[-1].start()
    for read, (q, i) in zip(reads, places):
        read.wait()
        rows = pl.ds(i * step, step)
        cols = pl.ds((q % COLUMN_PARTS) * part, part)
        wide[q, rows, :] = narrow[q, rows, :].astype(F32)
        out = grad_self if q // COLUMN_PARTS == 0 else grad_neigh
        writes.append(
            pltpu.make_async_copy(wide.at[q, rows], out.at[rows, cols], out_sems.at[q, i])
        )
        writes[-1].start()
    for c in writes:
        c.wait()


def body(nd, ns, features, w_self, w_neigh, cotangent, neighbours, hub_slots, send_rows, send_counts):
    verts, width = features.shape
    cap = send_rows.shape[2]
    hubs_own = hub_slots.shape[0]
    devices = nd * ns
    extra = round_up(hubs_own * devices + ns * cap, 128)
    picks = round_up(ns * cap + hubs_own, 16)
    pieces = 2 * COLUMN_PARTS
    part = width // COLUMN_PARTS
    plane = (nd // 2) * 2
    tall = ns // 2
    half = width // 2
    rows2 = half // plane
    scatter = rows2 % (tall * ROW_TILE) == 0
    rows3 = rows2 // tall if scatter else rows2
    landings = tall - 1 if scatter else tall
    most = max(plane, tall) - 1
    smem = pl.BlockSpec(memory_space=pltpu.SMEM)
    hbm = pl.BlockSpec(memory_space=pltpu.HBM)
    shapes = (
        jax.ShapeDtypeStruct((verts, width), BF),
        jax.ShapeDtypeStruct((verts, width), F32),
        jax.ShapeDtypeStruct((width, width), F32),
        jax.ShapeDtypeStruct((width, width), F32),
    )
    results = pl.pallas_call(
        functools.partial(kernel, nd, ns),
        out_shape=shapes[:2] + (jax.ShapeDtypeStruct((pieces, width, part), BF),),
        in_specs=[hbm] * 7 + [smem],
        out_specs=[hbm] * 3,
        scratch_shapes=[
            pltpu.VMEM((verts, width), BF),
            pltpu.VMEM((verts, width), F32),
            pltpu.VMEM((width, verts), BF),
            pltpu.SemaphoreType.DMA((2 + pieces,)),
            pltpu.VMEM((verts, width), BF),
            pltpu.VMEM((width, width), BF),
            pltpu.VMEM((width, width), BF),
            pltpu.VMEM((verts, width), BF),
            pltpu.VMEM((neighbours.shape[1], verts), jnp.int32),
            pltpu.SMEM((1, cap, ns), jnp.int32),
            pltpu.SMEM((1, ns), jnp.int32),
            pltpu.SemaphoreType.DMA((7,)),
            pltpu.VMEM((picks, verts), F32),
            pltpu.VMEM((picks, width), F32),
            pltpu.VMEM((hubs_own, width), F32),
            pltpu.VMEM((devices - 1, hubs_own, width), F32),
            pltpu.VMEM((ns, cap, width), F32),
            pltpu.VMEM((ns - 1, cap, width), F32),
            pltpu.VMEM((extra, width), F32),
            pltpu.VMEM((verts + extra, verts), BF),
            pltpu.VMEM((verts, width), BF),
            pltpu.VMEM((verts, width), F32),
            pltpu.VMEM((verts, width), BF),
            pltpu.VMEM((verts, width), BF),
            pltpu.VMEM((extra, width), F32),
            pltpu.VMEM((devices, hubs_own, width), F32),
            pltpu.VMEM((devices - 1, hubs_own, width), F32),
            pltpu.VMEM((ns, cap, width), F32),
            pltpu.VMEM((ns - 1, cap, width), F32),
            pltpu.VMEM((picks, width), F32),
            pltpu.VMEM((pieces, half, part), BF),
            pltpu.VMEM((pieces, half, part), BF),
            pltpu.VMEM((pieces, half, part), F32),
            pltpu.VMEM((pieces, plane - 1, rows2, part), BF),
            pltpu.VMEM((pieces, plane - 1, rows2, part), BF),
            pltpu.VMEM((pieces, rows2, part), F32),
            pltpu.VMEM((pieces, tall - 1, rows3, part), BF),
            pltpu.VMEM((pieces, landings, rows3, part), BF),
            pltpu.VMEM((pieces, width, part), BF),
            pltpu.SemaphoreType.DMA((4,)),
            pltpu.SemaphoreType.DMA((4,)),
            pltpu.SemaphoreType.DMA((pieces, 6, most)),
            pltpu.SemaphoreType.DMA((pieces, 6, most)),
        ],
        compiler_params=pltpu.CompilerParams(
            collective_id=0, has_side_effects=True, vmem_limit_bytes=VMEM_GRANT
        ),
    )(
        features, w_self, w_neigh, cotangent, neighbours.T, send_rows.transpose(0, 2, 1),
        send_counts, hub_slots,
    )
    return pl.pallas_call(
        writer,
        out_shape=shapes,
        in_specs=[hbm] * 3,
        out_specs=[hbm] * 4,
        scratch_shapes=[
            pltpu.VMEM((pieces, width, part), BF),
            pltpu.VMEM((pieces, width, part), F32),
            pltpu.VMEM((verts, width), BF),
            pltpu.VMEM((verts, width), F32),
            pltpu.SemaphoreType.DMA((pieces + 1, 2)),
            pltpu.SemaphoreType.DMA((pieces + 1, 2)),
        ],
        compiler_params=pltpu.CompilerParams(vmem_limit_bytes=VMEM_GRANT),
    )(*results)


def solution(mesh):
    both = ("dom", "shard")
    return jax.shard_map(
        functools.partial(body, mesh.shape["dom"], mesh.shape["shard"]),
        mesh=mesh,
        in_specs=(
            P(both, None),
            P(),
            P(),
            P(both, None),
            P(both, None),
            P(both),
            P(both, None, None),
            P(both, None),
        ),
        out_specs=(P(both, None), P(both, None), P(), P()),
        check_vma=False,
    )
```

```python
import functools

import jax
import jax.numpy as jnp
from jax import lax
from jax.experimental import pallas as pl
from jax.experimental.pallas import tpu as pltpu
from jax.sharding import PartitionSpec as P

BF = jnp.bfloat16
F32 = jnp.float32
MESH = pl.DeviceIdType.MESH
COLUMN_PARTS = 2
ROW_TILE = 16
VMEM_GRANT = 60 * 1024 * 1024


def contract_rows(left, right):
    return lax.dot_general(left, right, (((0,), (0,)), ((), ())), preferred_element_type=F32)


def contract_cols(left, right):
    return lax.dot_general(left, right, (((1,), (1,)), ((), ())), preferred_element_type=F32)


def dot(left, right):
    return jnp.dot(left, right, preferred_element_type=F32)


def round_up(value, step):
    return -(-value // step) * step


def kernel(
    nd, ns,
    features_hbm, w_self_hbm, w_neigh_hbm, cotangent_hbm, neighbours_hbm, rows_hbm, counts_hbm,
    hub_slots,
    hidden_hbm, grad_features_hbm, gathered_hbm,
    hidden, grad_features, features_t, store_sems,
    features, w_self, w_neigh, cotangent, neighbours, send_rows, send_counts, load_sems,
    pick, picked, hub_out, hub_in, bound_out, bound_in, table, count, agg, zs, dz, eg, accum,
    hub_send, hub_back, bound_send, bound_back, back,
    s1, r1, acc1, s2, r2, acc2, s3, r3, gathered,
    small_send, small_recv, send_sems, recv_sems,
):
    verts, width = features.shape
    slots = neighbours.shape[0]
    devices = nd * ns
    cap = send_rows.shape[1]
    hubs_own = hub_slots.shape[0]
    hub_count = hubs_own * devices
    live_rows = hub_count + ns * cap
    table_size = verts + live_rows
    dom = lax.axis_index("dom")
    shard = lax.axis_index("shard")
    me = dom * ns + shard
    core = lax.rem(dom, 2)
    y = lax.div(dom, 2)
    low = lax.rem(shard, 2)
    high = lax.div(shard, 2)

    def device_of(index):
        return (lax.div(index, ns), lax.rem(index, ns))

    pairs = (
        (rows_hbm, send_rows),
        (counts_hbm, send_counts),
        (features_hbm, features),
        (neighbours_hbm, neighbours),
        (w_self_hbm, w_self),
        (w_neigh_hbm, w_neigh),
        (cotangent_hbm, cotangent),
    )
    loads = [pltpu.make_async_copy(a, b, load_sems.at[i]) for i, (a, b) in enumerate(pairs)]
    for load in loads:
        load.start()

    barrier = pltpu.get_barrier_semaphore()

    def greet(k, carry):
        pl.semaphore_signal(
            barrier, inc=1, device_id=device_of(lax.rem(me + k, devices)), device_id_type=MESH
        )
        return carry

    lax.fori_loop(1, devices, greet, 0)

    lane = lax.broadcasted_iota(jnp.int32, (1, verts), 1)
    pick[...] = jnp.zeros_like(pick)
    loads[0].wait()
    loads[1].wait()
    for p in range(ns):
        for k in range(cap):
            row = jnp.where(k < send_counts[0, p], send_rows[0, k, p], -1)
            pick[pl.ds(p * cap + k, 1), :] = (lane == row).astype(F32)
    for h in range(hubs_own):
        pick[pl.ds(ns * cap + h, 1), :] = (lane == hub_slots[h]).astype(F32)
    loads[2].wait()
    picked[...] = dot(pick[...].astype(BF), features[...])
    for p in range(ns):
        bound_out[p] = picked[pl.ds(p * cap, cap), :]
    hub_out[...] = picked[pl.ds(ns * cap, hubs_own), :]

    pl.semaphore_wait(barrier, devices - 1)

    def hub_copy(k):
        return pltpu.make_async_remote_copy(
            src_ref=hub_out,
            dst_ref=hub_in.at[k - 1],
            send_sem=small_send.at[0],
            recv_sem=small_recv.at[0],
            device_id=device_of(lax.rem(me + k, devices)),
            device_id_type=MESH,
        )

    def hub_return(k):
        target = lax.rem(me + k, devices)
        return pltpu.make_async_remote_copy(
            src_ref=hub_send.at[target],
            dst_ref=hub_back.at[k - 1],
            send_sem=small_send.at[1],
            recv_sem=small_recv.at[1],
            device_id=device_of(target),
            device_id_type=MESH,
        )

    def bound_copy(source, landing, number):
        def make(k):
            target = lax.rem(shard + k, ns)
            return pltpu.make_async_remote_copy(
                src_ref=source.at[target],
                dst_ref=landing.at[k - 1],
                send_sem=small_send.at[number],
                recv_sem=small_recv.at[number],
                device_id=(dom, target),
                device_id_type=MESH,
            )

        return make

    def start_all(make, total):
        def one(k, carry):
            make(k).start()
            return carry

        lax.fori_loop(1, total, one, 0)

    def wait_all(landing, number):
        pltpu.make_async_copy(landing, landing, small_recv.at[number]).wait()
        pltpu.make_async_copy(landing, landing, small_send.at[number]).wait()

    start_all(bound_copy(bound_out, bound_in, 2), ns)
    start_all(hub_copy, devices)

    block = 64
    names = lax.broadcasted_iota(jnp.int32, (block, verts), 0)
    loads[3].wait()

    def count_block(i, carry):
        first = pl.multiple_of(i * block, block)
        total = jnp.zeros((block, verts), F32)
        for j in range(slots):
            total = total + (neighbours[pl.ds(j, 1), :] - first == names).astype(F32)
        count[pl.ds(first, block), :] = total.astype(BF)
        return carry

    lax.fori_loop(0, count.shape[0] // block, count_block, 0)
    alive = (neighbours[...] < table_size).astype(F32).astype(BF)
    degree = contract_rows(alive, jnp.ones((slots, 128), BF))
    inverse = jnp.concatenate([1.0 / degree] * (width // 128), axis=1)
    features_t[...] = features[...].T
    loads[4].wait()
    zs[...] = dot(features[...], w_self[...])
    local_sums = contract_rows(count[:verts, :], features[...])

    table[...] = jnp.zeros_like(table)
    for h in range(hubs_own):
        table[pl.ds(me * hubs_own + h, 1), :] = hub_out[pl.ds(h, 1), :]
    for k in range(cap):
        table[pl.ds(hub_count + shard * cap + k, 1), :] = bound_out[shard, pl.ds(k, 1), :]
    wait_all(bound_in, 2)
    for k in range(1, ns):
        source = lax.rem(shard - k + ns, ns)
        for i in range(cap):
            table[pl.ds(hub_count + source * cap + i, 1), :] = bound_in[k - 1, pl.ds(i, 1), :]
    wait_all(hub_in, 0)

    def place_hub(k, carry):
        source = lax.rem(me - k + devices, devices)
        for h in range(hubs_own):
            table[pl.ds(source * hubs_own + h, 1), :] = hub_in[k - 1, pl.ds(h, 1), :]
        return carry

    lax.fori_loop(1, devices, place_hub, 0)

    loads[5].wait()
    loads[6].wait()
    sums = local_sums + contract_rows(count[verts:, :], table[...].astype(BF))
    agg[...] = (sums * inverse).astype(BF)
    z = zs[...] + dot(agg[...], w_neigh[...])
    sig = jax.nn.sigmoid(z)
    hidden[...] = (z * sig).astype(BF)
    stores = [pltpu.make_async_copy(hidden, hidden_hbm, store_sems.at[0])]
    stores[0].start()
    dz[...] = (cotangent[...].astype(F32) * sig * (1.0 + z * (1.0 - sig))).astype(BF)

    part = width // COLUMN_PARTS
    pieces = 2 * COLUMN_PARTS
    plane = (nd // 2) * 2
    tall = ns // 2
    half = width // 2
    rows2 = half // plane
    scatter = rows2 % (tall * ROW_TILE) == 0
    rows3 = rows2 // tall if scatter else rows2
    my_plane = y * 2 + low
    base1 = core * half

    def at_core(j):
        return (y * 2 + j, shard)

    def at_plane(j):
        return (lax.div(j, 2) * 2 + core, high * 2 + lax.rem(j, 2))

    def at_tall(j):
        return (dom, j * 2 + low)

    def route(q):
        first, second = (plane, my_plane, at_plane), (tall, high, at_tall)
        if plane == tall and q == pieces // 2 and pieces > 2:
            return second, first
        return first, second

    def base2(q):
        return base1 + route(q)[0][1] * rows2

    def base3(q):
        return base2(q) + route(q)[1][1] * rows3 if scatter else base2(q)

    def copy(q, stage, k, source, landing, target):
        return pltpu.make_async_remote_copy(
            src_ref=source,
            dst_ref=landing,
            send_sem=send_sems.at[q, stage, k - 1],
            recv_sem=recv_sems.at[q, stage, k - 1],
            device_id=target,
            device_id_type=MESH,
        )

    def rows_at(start, size):
        return pl.ds(pl.multiple_of(start, ROW_TILE), size)

    def right_of(q):
        return dz[:, pl.ds((q % COLUMN_PARTS) * part, part)]

    def stage0(q):
        other = pl.ds(pl.multiple_of((1 - core) * half, half), half)
        own = pl.ds(pl.multiple_of(core * half, half), half)
        turned = q // COLUMN_PARTS == 0

        def product(rows):
            if turned:
                return dot(features_t[rows, :], right_of(q))
            return contract_rows(agg[:, rows], right_of(q))

        s1[q] = product(other).astype(BF)
        c = copy(q, 0, 1, s1.at[q], r1.at[q], at_core(1 - core))
        c.start()
        acc1[q] = product(own)
        return [c]

    def stage1(q):
        size, mine, at = route(q)[0]
        acc1[q] = acc1[q] + r1[q].astype(F32)
        copies = []
        for k in range(1, size):
            j = lax.rem(mine + k, size)
            s2[q, k - 1] = acc1[q, rows_at(j * rows2, rows2), :].astype(BF)
            c = copy(q, 1, k, s2.at[q, k - 1], r2.at[q, k - 1], at(j))
            c.start()
            copies.append(c)
        return copies

    def stage2(q):
        before, mine, _ = route(q)[0]
        total = acc1[q, rows_at(mine * rows2, rows2), :]
        for k in range(1, before):
            total = total + r2[q, k - 1].astype(F32)
        acc2[q] = total
        size, mine, at = route(q)[1]
        copies = []
        if not scatter:
            r3[q, mine] = total.astype(BF)
        for k in range(1, size):
            j = lax.rem(mine + k, size)
            if scatter:
                s3[q, k - 1] = acc2[q, rows_at(j * rows3, rows3), :].astype(BF)
                c = copy(q, 2, k, s3.at[q, k - 1], r3.at[q, k - 1], at(j))
            else:
                c = copy(q, 2, k, r3.at[q, mine], r3.at[q, mine], at(j))
            c.start()
            copies.append(c)
        return copies

    def stage3(q):
        size, mine, at = route(q)[1]
        if scatter:
            total = acc2[q, rows_at(mine * rows3, rows3), :]
            for k in range(1, size):
                total = total + r3[q, k - 1].astype(F32)
        else:
            total = r3[q, 0].astype(F32)
            for j in range(1, size):
                total = total + r3[q, j].astype(F32)
        gathered[q, rows_at(base3(q), rows3), :] = total.astype(BF)
        copies = []
        if scatter:
            chunk = gathered.at[q, rows_at(base3(q), rows3), :]
            for k in range(1, size):
                c = copy(q, 3, k, chunk, chunk, at(lax.rem(mine + k, size)))
                c.start()
                copies.append(c)
        return copies

    def stage4(q):
        size, mine, at = route(q)[0]
        chunk = gathered.at[q, rows_at(base2(q), rows2), :]
        copies = []
        for k in range(1, size):
            c = copy(q, 4, k, chunk, chunk, at(lax.rem(mine + k, size)))
            c.start()
            copies.append(c)
        return copies

    def stage5(q):
        chunk = gathered.at[q, rows_at(base1, half), :]
        c = copy(q, 5, 1, chunk, chunk, at_core(1 - core))
        c.start()
        return [c]

    def finish(copies):
        for c in copies:
            c.wait()

    stages = [stage0, stage1, stage2, stage3, stage4, stage5]
    def edge_gradients():
        eg[...] = (contract_cols(dz[...], w_neigh[...]) * inverse).astype(BF)
        accum[...] = dot(count[verts:, :], eg[...])

    def send_gradients():
        def fill(d, carry):
            for h in range(hubs_own):
                hub_send[d, pl.ds(h, 1), :] = accum[pl.ds(d * hubs_own + h, 1), :]
            return carry

        lax.fori_loop(0, devices, fill, 0)
        for p in range(ns):
            bound_send[p] = accum[pl.ds(hub_count + p * cap, cap), :]
        start_all(bound_copy(bound_send, bound_back, 3), ns)
        start_all(hub_return, devices)

    def own_gradients():
        grad_features[...] = contract_cols(dz[...], w_self[...]) + dot(count[:verts, :], eg[...])

    def take_gradients():
        back[...] = jnp.zeros_like(back)
        for i in range(cap):
            back[pl.ds(shard * cap + i, 1), :] = bound_send[shard, pl.ds(i, 1), :]
        wait_all(bound_back, 3)
        for k in range(1, ns):
            source = lax.rem(shard - k + ns, ns)
            for i in range(cap):
                back[pl.ds(source * cap + i, 1), :] = bound_back[k - 1, pl.ds(i, 1), :]
        wait_all(hub_back, 1)
        back[pl.ds(ns * cap, hubs_own), :] = hub_send[me] + jnp.sum(hub_back[...], axis=0)
        grad_features[...] = grad_features[...] + contract_rows(
            pick[...].astype(BF), back[...].astype(BF)
        )
        stores.append(pltpu.make_async_copy(grad_features, grad_features_hbm, store_sems.at[1]))
        stores[-1].start()

    flying = [stage0(0)]
    for q in range(pieces):
        if q + 1 < pieces:
            flying.append(stage0(q + 1))
        finish(flying[q])
        flying[q] = stage1(q)
    edge_gradients()
    steps = [(8 * number + 5 * q, number, q) for number in range(2, 6) for q in range(pieces)]
    for _, number, q in sorted(steps):
        finish(flying[q])
        flying[q] = stages[number](q)
        if (number, q) == (2, 1):
            send_gradients()
        if (number, q) == (2, pieces - 1):
            own_gradients()
        if (number, q) == (4, pieces - 1):
            take_gradients()
    for q in range(pieces):
        finish(flying[q])
        stores.append(
            pltpu.make_async_copy(gathered.at[q], gathered_hbm.at[q], store_sems.at[2 + q])
        )
        stores[-1].start()
    for store in stores:
        store.wait()


def writer(
    hidden_in, grad_features_in, gathered_in, hidden, grad_features, grad_self, grad_neigh,
    narrow, wide, hidden_held, grad_held, in_sems, out_sems,
):
    pieces, width, part = narrow.shape
    cuts = in_sems.shape[1]
    step = width // cuts
    places = [(q, i) for q in range(pieces) for i in range(cuts)]
    passed = (
        (hidden_in, hidden_held, hidden),
        (grad_features_in, grad_held, grad_features),
    )
    writes = []
    for i, (a, b, c) in enumerate(passed):
        pltpu.make_async_copy(a, b, in_sems.at[pieces, i]).start()
    reads = []
    for q, i in places:
        rows = pl.ds(i * step, step)
        reads.append(
            pltpu.make_async_copy(gathered_in.at[q, rows], narrow.at[q, rows], in_sems.at[q, i])
        )
        reads[-1].start()
    for i, (a, b, c) in enumerate(passed):
        pltpu.make_async_copy(a, b, in_sems.at[pieces, i]).wait()
        writes.append(pltpu.make_async_copy(b, c, out_sems.at[pieces, i]))
        writes[-1].start()
    for read, (q, i) in zip(reads, places):
        read.wait()
        rows = pl.ds(i * step, step)
        cols = pl.ds((q % COLUMN_PARTS) * part, part)
        wide[q, rows, :] = narrow[q, rows, :].astype(F32)
        out = grad_self if q // COLUMN_PARTS == 0 else grad_neigh
        writes.append(
            pltpu.make_async_copy(wide.at[q, rows], out.at[rows, cols], out_sems.at[q, i])
        )
        writes[-1].start()
    for c in writes:
        c.wait()


def body(nd, ns, features, w_self, w_neigh, cotangent, neighbours, hub_slots, send_rows, send_counts):
    verts, width = features.shape
    cap = send_rows.shape[2]
    hubs_own = hub_slots.shape[0]
    devices = nd * ns
    extra = round_up(hubs_own * devices + ns * cap, 128)
    picks = round_up(ns * cap + hubs_own, 16)
    pieces = 2 * COLUMN_PARTS
    part = width // COLUMN_PARTS
    plane = (nd // 2) * 2
    tall = ns // 2
    half = width // 2
    rows2 = half // plane
    scatter = rows2 % (tall * ROW_TILE) == 0
    rows3 = rows2 // tall if scatter else rows2
    landings = tall - 1 if scatter else tall
    most = max(plane, tall) - 1
    smem = pl.BlockSpec(memory_space=pltpu.SMEM)
    hbm = pl.BlockSpec(memory_space=pltpu.HBM)
    shapes = (
        jax.ShapeDtypeStruct((verts, width), BF),
        jax.ShapeDtypeStruct((verts, width), F32),
        jax.ShapeDtypeStruct((width, width), F32),
        jax.ShapeDtypeStruct((width, width), F32),
    )
    results = pl.pallas_call(
        functools.partial(kernel, nd, ns),
        out_shape=shapes[:2] + (jax.ShapeDtypeStruct((pieces, width, part), BF),),
        in_specs=[hbm] * 7 + [smem],
        out_specs=[hbm] * 3,
        scratch_shapes=[
            pltpu.VMEM((verts, width), BF),
            pltpu.VMEM((verts, width), F32),
            pltpu.VMEM((width, verts), BF),
            pltpu.SemaphoreType.DMA((2 + pieces,)),
            pltpu.VMEM((verts, width), BF),
            pltpu.VMEM((width, width), BF),
            pltpu.VMEM((width, width), BF),
            pltpu.VMEM((verts, width), BF),
            pltpu.VMEM((neighbours.shape[1], verts), jnp.int32),
            pltpu.SMEM((1, cap, ns), jnp.int32),
            pltpu.SMEM((1, ns), jnp.int32),
            pltpu.SemaphoreType.DMA((7,)),
            pltpu.VMEM((picks, verts), F32),
            pltpu.VMEM((picks, width), F32),
            pltpu.VMEM((hubs_own, width), F32),
            pltpu.VMEM((devices - 1, hubs_own, width), F32),
            pltpu.VMEM((ns, cap, width), F32),
            pltpu.VMEM((ns - 1, cap, width), F32),
            pltpu.VMEM((extra, width), F32),
            pltpu.VMEM((verts + extra, verts), BF),
            pltpu.VMEM((verts, width), BF),
            pltpu.VMEM((verts, width), F32),
            pltpu.VMEM((verts, width), BF),
            pltpu.VMEM((verts, width), BF),
            pltpu.VMEM((extra, width), F32),
            pltpu.VMEM((devices, hubs_own, width), F32),
            pltpu.VMEM((devices - 1, hubs_own, width), F32),
            pltpu.VMEM((ns, cap, width), F32),
            pltpu.VMEM((ns - 1, cap, width), F32),
            pltpu.VMEM((picks, width), F32),
            pltpu.VMEM((pieces, half, part), BF),
            pltpu.VMEM((pieces, half, part), BF),
            pltpu.VMEM((pieces, half, part), F32),
            pltpu.VMEM((pieces, plane - 1, rows2, part), BF),
            pltpu.VMEM((pieces, plane - 1, rows2, part), BF),
            pltpu.VMEM((pieces, rows2, part), F32),
            pltpu.VMEM((pieces, tall - 1, rows3, part), BF),
            pltpu.VMEM((pieces, landings, rows3, part), BF),
            pltpu.VMEM((pieces, width, part), BF),
            pltpu.SemaphoreType.DMA((4,)),
            pltpu.SemaphoreType.DMA((4,)),
            pltpu.SemaphoreType.DMA((pieces, 6, most)),
            pltpu.SemaphoreType.DMA((pieces, 6, most)),
        ],
        compiler_params=pltpu.CompilerParams(
            collective_id=0, has_side_effects=True, vmem_limit_bytes=VMEM_GRANT
        ),
    )(
        features, w_self, w_neigh, cotangent, neighbours.T, send_rows.transpose(0, 2, 1),
        send_counts, hub_slots,
    )
    return pl.pallas_call(
        writer,
        out_shape=shapes,
        in_specs=[hbm] * 3,
        out_specs=[hbm] * 4,
        scratch_shapes=[
            pltpu.VMEM((pieces, width, part), BF),
            pltpu.VMEM((pieces, width, part), F32),
            pltpu.VMEM((verts, width), BF),
            pltpu.VMEM((verts, width), F32),
            pltpu.SemaphoreType.DMA((pieces + 1, 2)),
            pltpu.SemaphoreType.DMA((pieces + 1, 2)),
        ],
        compiler_params=pltpu.CompilerParams(vmem_limit_bytes=VMEM_GRANT),
    )(*results)


def solution(mesh):
    both = ("dom", "shard")
    return jax.shard_map(
        functools.partial(body, mesh.shape["dom"], mesh.shape["shard"]),
        mesh=mesh,
        in_specs=(
            P(both, None),
            P(),
            P(),
            P(both, None),
            P(both, None),
            P(both),
            P(both, None, None),
            P(both, None),
        ),
        out_specs=(P(both, None), P(both, None), P(), P()),
        check_vma=False,
    )
```

```python
import functools

import jax
import jax.numpy as jnp
from jax import lax
from jax.experimental import pallas as pl
from jax.experimental.pallas import tpu as pltpu
from jax.sharding import PartitionSpec as P

BF = jnp.bfloat16
F32 = jnp.float32
MESH = pl.DeviceIdType.MESH
COLUMN_PARTS = 2
ROW_TILE = 16
VMEM_GRANT = 60 * 1024 * 1024


def contract_rows(left, right):
    return lax.dot_general(left, right, (((0,), (0,)), ((), ())), preferred_element_type=F32)


def contract_cols(left, right):
    return lax.dot_general(left, right, (((1,), (1,)), ((), ())), preferred_element_type=F32)


def dot(left, right):
    return jnp.dot(left, right, preferred_element_type=F32)


def round_up(value, step):
    return -(-value // step) * step


def kernel(
    nd, ns,
    features_hbm, w_self_hbm, w_neigh_hbm, cotangent_hbm, neighbours_hbm, rows_hbm, counts_hbm,
    hub_slots,
    hidden_hbm, grad_features_hbm, gathered_hbm,
    hidden, grad_features, features_t, store_sems,
    features, w_self, w_neigh, cotangent, neighbours, send_rows, send_counts, load_sems,
    pick, picked, hub_out, hub_in, bound_out, bound_in, table, count, agg, zs, dz, eg, accum,
    hub_send, hub_back, bound_send, bound_back, back,
    s1, r1, acc1, s2, r2, acc2, s3, r3, gathered,
    small_send, small_recv, send_sems, recv_sems,
):
    verts, width = features.shape
    slots = neighbours.shape[0]
    devices = nd * ns
    cap = send_rows.shape[1]
    hubs_own = hub_slots.shape[0]
    hub_count = hubs_own * devices
    live_rows = hub_count + ns * cap
    table_size = verts + live_rows
    dom = lax.axis_index("dom")
    shard = lax.axis_index("shard")
    me = dom * ns + shard
    core = lax.rem(dom, 2)
    y = lax.div(dom, 2)
    low = lax.rem(shard, 2)
    high = lax.div(shard, 2)

    def device_of(index):
        return (lax.div(index, ns), lax.rem(index, ns))

    pairs = (
        (rows_hbm, send_rows),
        (counts_hbm, send_counts),
        (features_hbm, features),
        (neighbours_hbm, neighbours),
        (w_self_hbm, w_self),
        (w_neigh_hbm, w_neigh),
        (cotangent_hbm, cotangent),
    )
    loads = [pltpu.make_async_copy(a, b, load_sems.at[i]) for i, (a, b) in enumerate(pairs)]
    for load in loads:
        load.start()

    barrier = pltpu.get_barrier_semaphore()

    def greet(k, carry):
        pl.semaphore_signal(
            barrier, inc=1, device_id=device_of(lax.rem(me + k, devices)), device_id_type=MESH
        )
        return carry

    lax.fori_loop(1, devices, greet, 0)

    lane = lax.broadcasted_iota(jnp.int32, (1, verts), 1)
    pick[...] = jnp.zeros_like(pick)
    loads[0].wait()
    loads[1].wait()
    for p in range(ns):
        for k in range(cap):
            row = jnp.where(k < send_counts[0, p], send_rows[0, k, p], -1)
            pick[pl.ds(p * cap + k, 1), :] = (lane == row).astype(F32)
    for h in range(hubs_own):
        pick[pl.ds(ns * cap + h, 1), :] = (lane == hub_slots[h]).astype(F32)
    loads[2].wait()
    picked[...] = dot(pick[...].astype(BF), features[...])
    for p in range(ns):
        bound_out[p] = picked[pl.ds(p * cap, cap), :]
    hub_out[...] = picked[pl.ds(ns * cap, hubs_own), :]

    pl.semaphore_wait(barrier, devices - 1)

    def hub_copy(k):
        return pltpu.make_async_remote_copy(
            src_ref=hub_out,
            dst_ref=hub_in.at[k - 1],
            send_sem=small_send.at[0],
            recv_sem=small_recv.at[0],
            device_id=device_of(lax.rem(me + k, devices)),
            device_id_type=MESH,
        )

    def hub_return(k):
        target = lax.rem(me + k, devices)
        return pltpu.make_async_remote_copy(
            src_ref=hub_send.at[target],
            dst_ref=hub_back.at[k - 1],
            send_sem=small_send.at[1],
            recv_sem=small_recv.at[1],
            device_id=device_of(target),
            device_id_type=MESH,
        )

    def bound_copy(source, landing, number):
        def make(k):
            target = lax.rem(shard + k, ns)
            return pltpu.make_async_remote_copy(
                src_ref=source.at[target],
                dst_ref=landing.at[k - 1],
                send_sem=small_send.at[number],
                recv_sem=small_recv.at[number],
                device_id=(dom, target),
                device_id_type=MESH,
            )

        return make

    def start_all(make, total):
        def one(k, carry):
            make(k).start()
            return carry

        lax.fori_loop(1, total, one, 0)

    def wait_all(landing, number):
        pltpu.make_async_copy(landing, landing, small_recv.at[number]).wait()
        pltpu.make_async_copy(landing, landing, small_send.at[number]).wait()

    start_all(bound_copy(bound_out, bound_in, 2), ns)
    start_all(hub_copy, devices)

    block = 64
    names = lax.broadcasted_iota(jnp.int32, (block, verts), 0)
    loads[3].wait()

    def count_block(i, carry):
        first = pl.multiple_of(i * block, block)
        total = jnp.zeros((block, verts), F32)
        for j in range(slots):
            total = total + (neighbours[pl.ds(j, 1), :] - first == names).astype(F32)
        count[pl.ds(first, block), :] = total.astype(BF)
        return carry

    lax.fori_loop(0, count.shape[0] // block, count_block, 0)
    alive = (neighbours[...] < table_size).astype(F32).astype(BF)
    degree = contract_rows(alive, jnp.ones((slots, 128), BF))
    inverse = jnp.concatenate([1.0 / degree] * (width // 128), axis=1)
    features_t[...] = features[...].T
    loads[4].wait()
    zs[...] = dot(features[...], w_self[...])
    local_sums = contract_rows(count[:verts, :], features[...])

    table[...] = jnp.zeros_like(table)
    for h in range(hubs_own):
        table[pl.ds(me * hubs_own + h, 1), :] = hub_out[pl.ds(h, 1), :]
    for k in range(cap):
        table[pl.ds(hub_count + shard * cap + k, 1), :] = bound_out[shard, pl.ds(k, 1), :]
    wait_all(bound_in, 2)
    for k in range(1, ns):
        source = lax.rem(shard - k + ns, ns)
        for i in range(cap):
            table[pl.ds(hub_count + source * cap + i, 1), :] = bound_in[k - 1, pl.ds(i, 1), :]
    wait_all(hub_in, 0)

    def place_hub(k, carry):
        source = lax.rem(me - k + devices, devices)
        for h in range(hubs_own):
            table[pl.ds(source * hubs_own + h, 1), :] = hub_in[k - 1, pl.ds(h, 1), :]
        return carry

    lax.fori_loop(1, devices, place_hub, 0)

    loads[5].wait()
    loads[6].wait()
    sums = local_sums + contract_rows(count[verts:, :], table[...].astype(BF))
    agg[...] = (sums * inverse).astype(BF)
    z = zs[...] + dot(agg[...], w_neigh[...])
    sig = jax.nn.sigmoid(z)
    hidden[...] = (z * sig).astype(BF)
    stores = [pltpu.make_async_copy(hidden, hidden_hbm, store_sems.at[0])]
    stores[0].start()
    dz[...] = (cotangent[...].astype(F32) * sig * (1.0 + z * (1.0 - sig))).astype(BF)

    part = width // COLUMN_PARTS
    pieces = 2 * COLUMN_PARTS
    plane = (nd // 2) * 2
    tall = ns // 2
    half = width // 2
    rows2 = half // plane
    scatter = rows2 % (tall * ROW_TILE) == 0
    rows3 = rows2 // tall if scatter else rows2
    my_plane = y * 2 + low
    base1 = core * half

    def at_core(j):
        return (y * 2 + j, shard)

    def at_plane(j):
        return (lax.div(j, 2) * 2 + core, high * 2 + lax.rem(j, 2))

    def at_tall(j):
        return (dom, j * 2 + low)

    def route(q):
        first, second = (plane, my_plane, at_plane), (tall, high, at_tall)
        if plane == tall and q == pieces // 2 and pieces > 2:
            return second, first
        return first, second

    def base2(q):
        return base1 + route(q)[0][1] * rows2

    def base3(q):
        return base2(q) + route(q)[1][1] * rows3 if scatter else base2(q)

    def copy(q, stage, k, source, landing, target):
        return pltpu.make_async_remote_copy(
            src_ref=source,
            dst_ref=landing,
            send_sem=send_sems.at[q, stage, k - 1],
            recv_sem=recv_sems.at[q, stage, k - 1],
            device_id=target,
            device_id_type=MESH,
        )

    def rows_at(start, size):
        return pl.ds(pl.multiple_of(start, ROW_TILE), size)

    def right_of(q):
        return dz[:, pl.ds((q % COLUMN_PARTS) * part, part)]

    def stage0(q):
        other = pl.ds(pl.multiple_of((1 - core) * half, half), half)
        own = pl.ds(pl.multiple_of(core * half, half), half)
        turned = q // COLUMN_PARTS == 0

        def product(rows):
            if turned:
                return dot(features_t[rows, :], right_of(q))
            return contract_rows(agg[:, rows], right_of(q))

        s1[q] = product(other).astype(BF)
        c = copy(q, 0, 1, s1.at[q], r1.at[q], at_core(1 - core))
        c.start()
        acc1[q] = product(own)
        return [c]

    def stage1(q):
        size, mine, at = route(q)[0]
        acc1[q] = acc1[q] + r1[q].astype(F32)
        copies = []
        for k in range(1, size):
            j = lax.rem(mine + k, size)
            s2[q, k - 1] = acc1[q, rows_at(j * rows2, rows2), :].astype(BF)
            c = copy(q, 1, k, s2.at[q, k - 1], r2.at[q, k - 1], at(j))
            c.start()
            copies.append(c)
        return copies

    def stage2(q):
        before, mine, _ = route(q)[0]
        total = acc1[q, rows_at(mine * rows2, rows2), :]
        for k in range(1, before):
            total = total + r2[q, k - 1].astype(F32)
        acc2[q] = total
        size, mine, at = route(q)[1]
        copies = []
        if not scatter:
            r3[q, mine] = total.astype(BF)
        for k in range(1, size):
            j = lax.rem(mine + k, size)
            if scatter:
                s3[q, k - 1] = acc2[q, rows_at(j * rows3, rows3), :].astype(BF)
                c = copy(q, 2, k, s3.at[q, k - 1], r3.at[q, k - 1], at(j))
            else:
                c = copy(q, 2, k, r3.at[q, mine], r3.at[q, mine], at(j))
            c.start()
            copies.append(c)
        return copies

    def stage3(q):
        size, mine, at = route(q)[1]
        if scatter:
            total = acc2[q, rows_at(mine * rows3, rows3), :]
            for k in range(1, size):
                total = total + r3[q, k - 1].astype(F32)
        else:
            total = r3[q, 0].astype(F32)
            for j in range(1, size):
                total = total + r3[q, j].astype(F32)
        gathered[q, rows_at(base3(q), rows3), :] = total.astype(BF)
        copies = []
        if scatter:
            chunk = gathered.at[q, rows_at(base3(q), rows3), :]
            for k in range(1, size):
                c = copy(q, 3, k, chunk, chunk, at(lax.rem(mine + k, size)))
                c.start()
                copies.append(c)
        return copies

    def stage4(q):
        size, mine, at = route(q)[0]
        chunk = gathered.at[q, rows_at(base2(q), rows2), :]
        copies = []
        for k in range(1, size):
            c = copy(q, 4, k, chunk, chunk, at(lax.rem(mine + k, size)))
            c.start()
            copies.append(c)
        return copies

    def stage5(q):
        chunk = gathered.at[q, rows_at(base1, half), :]
        c = copy(q, 5, 1, chunk, chunk, at_core(1 - core))
        c.start()
        return [c]

    def finish(copies):
        for c in copies:
            c.wait()

    stages = [stage0, stage1, stage2, stage3, stage4, stage5]
    def edge_gradients():
        eg[...] = (contract_cols(dz[...], w_neigh[...]) * inverse).astype(BF)
        accum[...] = dot(count[verts:, :], eg[...])

    def send_gradients():
        def fill(d, carry):
            for h in range(hubs_own):
                hub_send[d, pl.ds(h, 1), :] = accum[pl.ds(d * hubs_own + h, 1), :]
            return carry

        lax.fori_loop(0, devices, fill, 0)
        for p in range(ns):
            bound_send[p] = accum[pl.ds(hub_count + p * cap, cap), :]
        start_all(bound_copy(bound_send, bound_back, 3), ns)
        start_all(hub_return, devices)

    def own_gradients():
        grad_features[...] = contract_cols(dz[...], w_self[...]) + dot(count[:verts, :], eg[...])

    def take_gradients():
        back[...] = jnp.zeros_like(back)
        for i in range(cap):
            back[pl.ds(shard * cap + i, 1), :] = bound_send[shard, pl.ds(i, 1), :]
        wait_all(bound_back, 3)
        for k in range(1, ns):
            source = lax.rem(shard - k + ns, ns)
            for i in range(cap):
                back[pl.ds(source * cap + i, 1), :] = bound_back[k - 1, pl.ds(i, 1), :]
        wait_all(hub_back, 1)
        back[pl.ds(ns * cap, hubs_own), :] = hub_send[me] + jnp.sum(hub_back[...], axis=0)
        grad_features[...] = grad_features[...] + contract_rows(
            pick[...].astype(BF), back[...].astype(BF)
        )
        stores.append(pltpu.make_async_copy(grad_features, grad_features_hbm, store_sems.at[1]))
        stores[-1].start()

    flying = [stage0(0)]
    for q in range(pieces):
        if q + 1 < pieces:
            flying.append(stage0(q + 1))
        finish(flying[q])
        flying[q] = stage1(q)
    edge_gradients()
    steps = [(pieces * number + q, number, q) for number in range(2, 6) for q in range(pieces)]
    for _, number, q in sorted(steps):
        finish(flying[q])
        flying[q] = stages[number](q)
        if (number, q) == (2, 0):
            send_gradients()
        if (number, q) == (2, pieces - 1):
            own_gradients()
        if (number, q) == (4, pieces - 1):
            take_gradients()
    for q in range(pieces):
        finish(flying[q])
        stores.append(
            pltpu.make_async_copy(gathered.at[q], gathered_hbm.at[q], store_sems.at[2 + q])
        )
        stores[-1].start()
    for store in stores:
        store.wait()


def writer(
    hidden_in, grad_features_in, gathered_in, hidden, grad_features, grad_self, grad_neigh,
    narrow, wide, hidden_held, grad_held, in_sems, out_sems,
):
    pieces, width, part = narrow.shape
    cuts = in_sems.shape[1]
    step = width // cuts
    places = [(q, i) for q in range(pieces) for i in range(cuts)]
    passed = (
        (hidden_in, hidden_held, hidden),
        (grad_features_in, grad_held, grad_features),
    )
    writes = []
    for i, (a, b, c) in enumerate(passed):
        pltpu.make_async_copy(a, b, in_sems.at[pieces, i]).start()
    reads = []
    for q, i in places:
        rows = pl.ds(i * step, step)
        reads.append(
            pltpu.make_async_copy(gathered_in.at[q, rows], narrow.at[q, rows], in_sems.at[q, i])
        )
        reads[-1].start()
    for i, (a, b, c) in enumerate(passed):
        pltpu.make_async_copy(a, b, in_sems.at[pieces, i]).wait()
        writes.append(pltpu.make_async_copy(b, c, out_sems.at[pieces, i]))
        writes[-1].start()
    for read, (q, i) in zip(reads, places):
        read.wait()
        rows = pl.ds(i * step, step)
        cols = pl.ds((q % COLUMN_PARTS) * part, part)
        wide[q, rows, :] = narrow[q, rows, :].astype(F32)
        out = grad_self if q // COLUMN_PARTS == 0 else grad_neigh
        writes.append(
            pltpu.make_async_copy(wide.at[q, rows], out.at[rows, cols], out_sems.at[q, i])
        )
        writes[-1].start()
    for c in writes:
        c.wait()


def body(nd, ns, features, w_self, w_neigh, cotangent, neighbours, hub_slots, send_rows, send_counts):
    verts, width = features.shape
    cap = send_rows.shape[2]
    hubs_own = hub_slots.shape[0]
    devices = nd * ns
    extra = round_up(hubs_own * devices + ns * cap, 128)
    picks = round_up(ns * cap + hubs_own, 16)
    pieces = 2 * COLUMN_PARTS
    part = width // COLUMN_PARTS
    plane = (nd // 2) * 2
    tall = ns // 2
    half = width // 2
    rows2 = half // plane
    scatter = rows2 % (tall * ROW_TILE) == 0
    rows3 = rows2 // tall if scatter else rows2
    landings = tall - 1 if scatter else tall
    most = max(plane, tall) - 1
    smem = pl.BlockSpec(memory_space=pltpu.SMEM)
    hbm = pl.BlockSpec(memory_space=pltpu.HBM)
    shapes = (
        jax.ShapeDtypeStruct((verts, width), BF),
        jax.ShapeDtypeStruct((verts, width), F32),
        jax.ShapeDtypeStruct((width, width), F32),
        jax.ShapeDtypeStruct((width, width), F32),
    )
    results = pl.pallas_call(
        functools.partial(kernel, nd, ns),
        out_shape=shapes[:2] + (jax.ShapeDtypeStruct((pieces, width, part), BF),),
        in_specs=[hbm] * 7 + [smem],
        out_specs=[hbm] * 3,
        scratch_shapes=[
            pltpu.VMEM((verts, width), BF),
            pltpu.VMEM((verts, width), F32),
            pltpu.VMEM((width, verts), BF),
            pltpu.SemaphoreType.DMA((2 + pieces,)),
            pltpu.VMEM((verts, width), BF),
            pltpu.VMEM((width, width), BF),
            pltpu.VMEM((width, width), BF),
            pltpu.VMEM((verts, width), BF),
            pltpu.VMEM((neighbours.shape[1], verts), jnp.int32),
            pltpu.SMEM((1, cap, ns), jnp.int32),
            pltpu.SMEM((1, ns), jnp.int32),
            pltpu.SemaphoreType.DMA((7,)),
            pltpu.VMEM((picks, verts), F32),
            pltpu.VMEM((picks, width), F32),
            pltpu.VMEM((hubs_own, width), F32),
            pltpu.VMEM((devices - 1, hubs_own, width), F32),
            pltpu.VMEM((ns, cap, width), F32),
            pltpu.VMEM((ns - 1, cap, width), F32),
            pltpu.VMEM((extra, width), F32),
            pltpu.VMEM((verts + extra, verts), BF),
            pltpu.VMEM((verts, width), BF),
            pltpu.VMEM((verts, width), F32),
            pltpu.VMEM((verts, width), BF),
            pltpu.VMEM((verts, width), BF),
            pltpu.VMEM((extra, width), F32),
            pltpu.VMEM((devices, hubs_own, width), F32),
            pltpu.VMEM((devices - 1, hubs_own, width), F32),
            pltpu.VMEM((ns, cap, width), F32),
            pltpu.VMEM((ns - 1, cap, width), F32),
            pltpu.VMEM((picks, width), F32),
            pltpu.VMEM((pieces, half, part), BF),
            pltpu.VMEM((pieces, half, part), BF),
            pltpu.VMEM((pieces, half, part), F32),
            pltpu.VMEM((pieces, plane - 1, rows2, part), BF),
            pltpu.VMEM((pieces, plane - 1, rows2, part), BF),
            pltpu.VMEM((pieces, rows2, part), F32),
            pltpu.VMEM((pieces, tall - 1, rows3, part), BF),
            pltpu.VMEM((pieces, landings, rows3, part), BF),
            pltpu.VMEM((pieces, width, part), BF),
            pltpu.SemaphoreType.DMA((4,)),
            pltpu.SemaphoreType.DMA((4,)),
            pltpu.SemaphoreType.DMA((pieces, 6, most)),
            pltpu.SemaphoreType.DMA((pieces, 6, most)),
        ],
        compiler_params=pltpu.CompilerParams(
            collective_id=0, has_side_effects=True, vmem_limit_bytes=VMEM_GRANT
        ),
    )(
        features, w_self, w_neigh, cotangent, neighbours.T, send_rows.transpose(0, 2, 1),
        send_counts, hub_slots,
    )
    return pl.pallas_call(
        writer,
        out_shape=shapes,
        in_specs=[hbm] * 3,
        out_specs=[hbm] * 4,
        scratch_shapes=[
            pltpu.VMEM((pieces, width, part), BF),
            pltpu.VMEM((pieces, width, part), F32),
            pltpu.VMEM((verts, width), BF),
            pltpu.VMEM((verts, width), F32),
            pltpu.SemaphoreType.DMA((pieces + 1, 2)),
            pltpu.SemaphoreType.DMA((pieces + 1, 2)),
        ],
        compiler_params=pltpu.CompilerParams(vmem_limit_bytes=VMEM_GRANT),
    )(*results)


def solution(mesh):
    both = ("dom", "shard")
    return jax.shard_map(
        functools.partial(body, mesh.shape["dom"], mesh.shape["shard"]),
        mesh=mesh,
        in_specs=(
            P(both, None),
            P(),
            P(),
            P(both, None),
            P(both, None),
            P(both),
            P(both, None, None),
            P(both, None),
        ),
        out_specs=(P(both, None), P(both, None), P(), P()),
        check_vma=False,
    )
```
